32 devices in a mesh: seq: 16 (over z, y, core), kvh: 2 (over x).
Axes of the slice: x: 2, y: 2, z: 4, core: 2. Of those that a mesh axis runs over, the one named last changes fastest.
Arguments:
- queries: bfloat16 [4096, 2048], P('seq', 'kvh'), may hold values from -2.5 to 2.5
- key_vector_rows: bfloat16 [4096, 256], P(('seq', 'kvh')), may hold values from -2.5 to 2.5
- value_vector_rows: bfloat16 [4096, 256], P(('seq', 'kvh')), may hold values from -5 to 5
- output_gradient: bfloat16 [4096, 2048], P('seq', 'kvh'), may hold values from -24 to 24
- key_lists: int32 [32, 24], replicated, may hold values from 0 to 31, as said below
- block_counts: int32 [32], replicated, may hold values from 1 to 24, as said below
- span_table: int32 [32], replicated, may hold values from 0 to 31, each once
Outputs:
- grad_queries: bfloat16 [4096, 2048], P('seq', 'kvh')
- key_gradient: bfloat16 [4096, 256], P(('seq', 'kvh'))
- value_gradient: bfloat16 [4096, 256], P(('seq', 'kvh'))
The draws below stay inside these ranges and needn't reach their ends.
Inputs may be any that keep to these rules, and one draw needn't show every extreme that they name: `key_lists`: row b lists, by position, the key blocks of query block b: its first block_counts[b] entries are distinct blocks at or before b, the first being b itself; the remaining entries are 0. block_counts[b] is at most b + 1 and at most 24; the last block's count is 24. `span_table`: each position block appears once.
All inputs are finite; a program needn't handle non-finite values.
Results may differ from the reference program's by a relative error of at most 0.0055.
Values may be sent and summed in bfloat16 or wider, within the bound.
No kernel may reach another device: no remote copies, remote signals or barrier semaphores. Data moves between devices by JAX's collectives and lax.ppermute only.
A program may use at most 128 MiB of HBM per device.

```python
import jax
import jax.numpy as jnp
from jax import lax

HEAD_SIZE = 128
QUERY_PER_KEY = 8
BLOCK_TOKENS = 128
NB = 24
BLOCK_COUNT = 32
TRAJECTORY_LEN = 4096
KEY_VALUE_HEADS = 2
HQ = 16


def lists_and_counts(key):
    base_key = jax.random.fold_in(key, 11)
    first_key, second_key = jax.random.split(base_key)
    block_ids = jnp.arange(BLOCK_COUNT, dtype=jnp.int32)
    limits = jax.random.randint(first_key, (BLOCK_COUNT,), (NB + 1) // 2, NB + 1, dtype=jnp.int32)
    limits = jnp.where(block_ids == BLOCK_COUNT - 1, NB, limits)
    counts_drawn = jnp.minimum(block_ids + 1, limits).astype(jnp.int32)
    columns = block_ids[None, :]
    random_rank = jax.random.randint(second_key, (BLOCK_COUNT, BLOCK_COUNT), 0, 1 << 20, dtype=jnp.int32)
    eligible = jnp.logical_and(columns >= 1, columns <= block_ids[:, None] - 2)
    ranked = jnp.where(eligible, random_rank * BLOCK_COUNT + columns, (1 << 30) + columns)
    chosen = lax.top_k(-ranked, NB)[1].astype(jnp.int32)
    fixed_part = jnp.stack([block_ids, block_ids - 1, jnp.zeros_like(block_ids)], 1)
    lists = jnp.concatenate([fixed_part, chosen[:, :NB - 3]], 1)
    entry_ids = jnp.arange(NB, dtype=jnp.int32)[None, :]
    lists = jnp.where(entry_ids < counts_drawn[:, None], lists, 0).astype(jnp.int32)
    return (lists, counts_drawn)


def draw_key_lists(key, part):
    return lists_and_counts(key)[0]


def draw_block_counts(key, part):
    return lists_and_counts(key)[1]


def shard_levels(stream_key, dims, shards, low, top_value):
    factor_of = 1.0
    for axis_at, shards_of in shards:
        heights = jax.random.uniform(jax.random.fold_in(jax.random.fold_in(stream_key, 6), axis_at), (shards_of,), jnp.float32, low / len(shards), top_value / len(shards))
        factor_of = factor_of * jnp.repeat(jnp.exp(heights), dims[axis_at] // shards_of).reshape((-1,) + (1,) * (len(dims) - 1 - axis_at))
    return factor_of


def normal_values(own_key, shape, spread, bound, cuts=(), held_as=jnp.bfloat16):
    result = spread * jax.random.normal(own_key, shape, jnp.float32)
    if cuts:
        result = result * shard_levels(own_key, shape, cuts, -0.22, 0.18)
    return jnp.clip(result, -bound, bound).astype(held_as)


def setup_inputs(seed: int = 0) -> dict:
    key_list = jax.random.split(jax.random.key(seed), 8)
    queries = normal_values(key_list[0], (TRAJECTORY_LEN, HQ * HEAD_SIZE), 1.0, 2.5, ((0, 16), (1, 2)))
    key_vector_rows = normal_values(key_list[1], (TRAJECTORY_LEN, KEY_VALUE_HEADS * HEAD_SIZE), 1.0, 2.5, ((0, 32),))
    value_vector_rows = normal_values(key_list[2], (TRAJECTORY_LEN, KEY_VALUE_HEADS * HEAD_SIZE), 1.0, 5.0, ((0, 32),))
    output_gradient = normal_values(key_list[3], (TRAJECTORY_LEN, HQ * HEAD_SIZE), 4.0, 24.0, ((0, 16), (1, 2)))
    key_lists = draw_key_lists(jax.random.fold_in(key_list[7], 71), 0)
    block_counts = draw_block_counts(jax.random.fold_in(key_list[7], 71), 0)
    span_table = jax.random.permutation(key_list[6], BLOCK_COUNT).astype(jnp.int32)
    return {"queries": queries, "key_vector_rows": key_vector_rows, "value_vector_rows": value_vector_rows, "output_gradient": output_gradient, "key_lists": key_lists, "block_counts": block_counts, "span_table": span_table}


def rounded(values_in):
    return lax.optimization_barrier(values_in.astype(jnp.bfloat16)).astype(jnp.float32)


def reference(queries, key_vector_rows, value_vector_rows, output_gradient, key_lists, block_counts, span_table):
    logit_scale = HEAD_SIZE ** -0.5
    blocked_queries = queries.astype(jnp.float32).reshape(BLOCK_COUNT, BLOCK_TOKENS, KEY_VALUE_HEADS, QUERY_PER_KEY, HEAD_SIZE)
    blocked_keys = key_vector_rows.astype(jnp.float32).reshape(BLOCK_COUNT, BLOCK_TOKENS, KEY_VALUE_HEADS, HEAD_SIZE)
    blocked_values = value_vector_rows.astype(jnp.float32).reshape(BLOCK_COUNT, BLOCK_TOKENS, KEY_VALUE_HEADS, HEAD_SIZE)
    gradient_block_list = output_gradient.astype(jnp.float32).reshape(BLOCK_COUNT, BLOCK_TOKENS, KEY_VALUE_HEADS, QUERY_PER_KEY, HEAD_SIZE)
    block_ids = jnp.arange(BLOCK_COUNT, dtype=jnp.int32)
    inverse = jnp.zeros((BLOCK_COUNT,), jnp.int32).at[span_table].set(block_ids)
    lower_mask = jnp.arange(BLOCK_TOKENS)[None, :] <= jnp.arange(BLOCK_TOKENS)[:, None]

    def slot_step(carried, slot):
        key_gradient_total, value_gradient_total = carried
        query_pos = span_table[slot]
        entries = block_counts[query_pos]
        query_blk = blocked_queries[slot]
        grad_blk = gradient_block_list[slot]

        def scored(entry_id):
            key_pos = key_lists[query_pos, entry_id]
            key_slot = inverse[key_pos]
            key_blk = blocked_keys[key_slot]
            value_blk = blocked_values[key_slot]
            scores = jnp.einsum("thgd,shd->hgts", query_blk, key_blk) * logit_scale
            allowed = jnp.logical_or(key_pos != query_pos, lower_mask)
            return scores, allowed, key_blk, value_blk, key_slot

        def forward_step(entry_id, state_pair):
            row_total, weighted = state_pair
            scores, allowed, key_blk, value_blk, key_slot = scored(entry_id)
            exp_scores = jnp.where(allowed, jnp.exp(scores), jnp.float32(0.0))
            row_total = row_total + jnp.sum(exp_scores, -1)
            weighted = weighted + jnp.einsum("hgts,shd->thgd", rounded(exp_scores), value_blk)
            return row_total, weighted

        starting_carry = (jnp.zeros((KEY_VALUE_HEADS, QUERY_PER_KEY, BLOCK_TOKENS), jnp.float32), jnp.zeros((BLOCK_TOKENS, KEY_VALUE_HEADS, QUERY_PER_KEY, HEAD_SIZE), jnp.float32))
        row_total, weighted = lax.fori_loop(0, entries, forward_step, starting_carry)
        log_total = jnp.log(row_total)
        attended = weighted / jnp.transpose(row_total, (2, 0, 1))[..., None]
        row_delta = jnp.transpose(jnp.sum(grad_blk * attended, -1), (1, 2, 0))

        def backward_step(entry_id, state_triple):
            query_grad, key_inner, value_inner = state_triple
            scores, allowed, key_blk, value_blk, key_slot = scored(entry_id)
            weights = jnp.where(allowed, jnp.exp(scores - log_total[..., None]), jnp.float32(0.0))
            value_part = jnp.einsum("hgts,thgd->shd", rounded(weights), grad_blk)
            weight_grads = jnp.einsum("thgd,shd->hgts", grad_blk, value_blk)
            score_grads = rounded(weights * (weight_grads - row_delta[..., None]))
            query_grad = query_grad + jnp.einsum("hgts,shd->thgd", score_grads, key_blk)
            key_part = jnp.einsum("hgts,thgd->shd", score_grads, query_blk)
            key_inner = key_inner.at[key_slot].add(key_part)
            value_inner = value_inner.at[key_slot].add(value_part)
            return query_grad, key_inner, value_inner

        initial_gradient = jnp.zeros((BLOCK_TOKENS, KEY_VALUE_HEADS, QUERY_PER_KEY, HEAD_SIZE), jnp.float32)
        query_grad, key_gradient_total, value_gradient_total = lax.fori_loop(0, entries, backward_step, (initial_gradient, key_gradient_total, value_gradient_total))
        return (key_gradient_total, value_gradient_total), (query_grad * logit_scale).astype(jnp.bfloat16)

    empty_totals = jnp.zeros((BLOCK_COUNT, BLOCK_TOKENS, KEY_VALUE_HEADS, HEAD_SIZE), jnp.float32)
    (key_gradient_total, value_gradient_total), query_out = lax.scan(slot_step, (empty_totals, empty_totals), block_ids)
    grad_queries = query_out.reshape(TRAJECTORY_LEN, HQ * HEAD_SIZE)
    key_gradient = (key_gradient_total * logit_scale).astype(jnp.bfloat16).reshape(TRAJECTORY_LEN, KEY_VALUE_HEADS * HEAD_SIZE)
    value_gradient = value_gradient_total.astype(jnp.bfloat16).reshape(TRAJECTORY_LEN, KEY_VALUE_HEADS * HEAD_SIZE)
    return (grad_queries, key_gradient, value_gradient)
```

```python
import functools

import jax
import jax.numpy as jnp
from jax import lax
from jax.experimental import pallas as pl
from jax.experimental.pallas import tpu as pltpu
from jax.sharding import PartitionSpec as P

HEAD = 128
GROUP = 8
BLOCK = 128
SCALE = HEAD ** (-0.5)
LOG2E = 1.4426950408889634
SCORE_SCALE = SCALE * LOG2E
TILE = 2 * BLOCK
WIDE = GROUP * BLOCK
BF16 = jnp.bfloat16
F32 = jnp.float32


def attend_kernel(
    counts,
    slots,
    qt_ref,
    dot_ref,
    qs_ref,
    dos_ref,
    kv_ref,
    dqt_ref,
    dkv_ref,
    kt_scr,
    total_scr,
    delta_scr,
    w_scr,
    ds_scr,
    acc_scr,
):
    local_blocks = qt_ref.shape[0]
    n_slots = kv_ref.shape[0] // BLOCK
    acc_scr[...] = jnp.zeros_like(acc_scr)
    dqt_ref[...] = jnp.zeros_like(dqt_ref)
    total_scr[...] = jnp.zeros_like(total_scr)
    delta_scr[...] = jnp.zeros_like(delta_scr)

    def turn(j, carry):
        rows = pl.ds(pl.multiple_of(j * BLOCK, BLOCK), BLOCK)
        kt_scr[j] = kv_ref[rows, :HEAD].T
        return carry

    lax.fori_loop(0, n_slots, turn, 0)

    def rows_of(i, entry):
        return pl.ds(pl.multiple_of(slots[i, entry] * BLOCK, BLOCK), BLOCK)

    def allowed(i, chunk):
        key_at = lax.broadcasted_iota(jnp.int32, (TILE, TILE), 0)
        query_at = lax.broadcasted_iota(jnp.int32, (TILE, TILE), 1) & (BLOCK - 1)
        second = key_at >= BLOCK
        entry = 2 * chunk + second.astype(jnp.int32)
        here = key_at & (BLOCK - 1)
        causal = jnp.logical_or(entry > 0, here <= query_at)
        return jnp.logical_and(entry < counts[i], causal)

    def pair(ref, i, chunk, lanes):
        return jnp.concatenate(
            [ref[rows_of(i, 2 * chunk), lanes], ref[rows_of(i, 2 * chunk + 1), lanes]], 0
        )

    def first_pass(i, chunk, masked):
        keys = pair(kv_ref, i, chunk, slice(0, HEAD))
        values = pair(kv_ref, i, chunk, slice(HEAD, 2 * HEAD))
        mask = allowed(i, chunk) if masked else None
        for h in range(0, WIDE, TILE):
            lanes = slice(h, h + TILE)
            scores = jnp.dot(keys, qt_ref[i, :, lanes], preferred_element_type=F32)
            expd = jnp.exp2(scores * SCORE_SCALE)
            if masked:
                expd = jnp.where(mask, expd, 0.0)
            total_scr[i, :, lanes] += jnp.sum(expd.reshape(TILE // 8, 8, TILE), 0)
            dweights = jnp.dot(values, dot_ref[i, :, lanes], preferred_element_type=F32)
            delta_scr[i, :, lanes] += jnp.sum((expd * dweights).reshape(TILE // 8, 8, TILE), 0)

    def second_pass(i, chunk, masked):
        keys = pair(kv_ref, i, chunk, slice(0, HEAD))
        values = pair(kv_ref, i, chunk, slice(HEAD, 2 * HEAD))
        mask = allowed(i, chunk) if masked else None
        keys_t = jnp.concatenate([kt_scr[slots[i, 2 * chunk]], kt_scr[slots[i, 2 * chunk + 1]]], 1)
        for h in range(0, WIDE, TILE):
            lanes = slice(h, h + TILE)
            scores = jnp.dot(keys, qt_ref[i, :, lanes], preferred_element_type=F32)
            weights = jnp.exp2(scores * SCORE_SCALE - total_scr[i, 0:1, lanes])
            if masked:
                weights = jnp.where(mask, weights, 0.0)
            dweights = jnp.dot(values, dot_ref[i, :, lanes], preferred_element_type=F32)
            dscores = (weights * (dweights - delta_scr[i, 0:1, lanes])).astype(BF16)
            w_scr[:, lanes] = weights.astype(BF16)
            ds_scr[:, lanes] = dscores
            dqt_ref[i, :, lanes] += jnp.dot(keys_t, dscores, preferred_element_type=F32)
        dk = jnp.dot(ds_scr[...], qs_ref[i], preferred_element_type=F32)
        dv = jnp.dot(w_scr[...], dos_ref[i], preferred_element_type=F32)
        for half in range(2):
            rows = rows_of(i, 2 * chunk + half)
            part = slice(half * BLOCK, (half + 1) * BLOCK)
            acc_scr[rows, :HEAD] += dk[part]
            acc_scr[rows, HEAD:] += dv[part]

    def sweep(i, step):
        chunks = (counts[i] + 1) // 2

        def body(chunk, carry):
            special = jnp.logical_or(chunk == 0, 2 * chunk + 2 > counts[i])

            @pl.when(special)
            def _():
                step(i, chunk, True)

            @pl.when(jnp.logical_not(special))
            def _():
                step(i, chunk, False)

            return carry

        lax.fori_loop(0, chunks, body, 0)

    def one_block(i, carry):
        sweep(i, first_pass)
        total = jnp.sum(total_scr[i], 0, keepdims=True)
        delta = jnp.sum(delta_scr[i], 0, keepdims=True) / total
        total_scr[i] = jnp.broadcast_to(jnp.log2(total), (8, WIDE))
        delta_scr[i] = jnp.broadcast_to(delta, (8, WIDE))
        sweep(i, second_pass)
        return carry

    lax.fori_loop(0, local_blocks, one_block, 0)
    dkv_ref[...] = acc_scr[...].astype(dkv_ref.dtype)


def attend(counts, slots, qt, dot, qs, dos, kv):
    local_blocks = qt.shape[0]
    smem = pl.BlockSpec(memory_space=pltpu.SMEM)
    vmem = pl.BlockSpec(memory_space=pltpu.VMEM)
    return pl.pallas_call(
        attend_kernel,
        in_specs=[smem, smem] + [vmem] * 5,
        out_specs=[vmem, vmem],
        out_shape=[
            jax.ShapeDtypeStruct((local_blocks, HEAD, WIDE), F32),
            jax.ShapeDtypeStruct(kv.shape, BF16),
        ],
        scratch_shapes=[
            pltpu.VMEM((kv.shape[0] // BLOCK, HEAD, BLOCK), BF16),
            pltpu.VMEM((local_blocks, 8, WIDE), F32),
            pltpu.VMEM((local_blocks, 8, WIDE), F32),
            pltpu.VMEM((TILE, WIDE), BF16),
            pltpu.VMEM((TILE, WIDE), BF16),
            pltpu.VMEM(kv.shape, F32),
        ],
        compiler_params=pltpu.CompilerParams(vmem_limit_bytes=48 << 20),
        name="attend",
    )(counts, slots, qt, dot, qs, dos, kv)


def shards(
    queries,
    key_vector_rows,
    value_vector_rows,
    output_gradient,
    key_lists,
    block_counts,
    span_table,
):
    local_blocks = queries.shape[0] // BLOCK
    kv_devices = lax.axis_size("kvh")
    per_kvh = key_vector_rows.shape[0]
    kv_rows = jnp.stack(
        [key_vector_rows.reshape(per_kvh, kv_devices, HEAD), value_vector_rows.reshape(per_kvh, kv_devices, HEAD)], 2
    )
    kv_rows = jnp.transpose(kv_rows, (1, 0, 2, 3)).reshape(kv_devices * per_kvh, 2 * HEAD)
    kv_head = lax.all_to_all(kv_rows, "kvh", split_axis=0, concat_axis=0, tiled=True)
    kv_all = lax.all_gather(kv_head, "seq", axis=0, tiled=True)

    first_slot = lax.axis_index("seq") * local_blocks
    positions = lax.dynamic_slice_in_dim(span_table, first_slot, local_blocks, 0)
    counts = block_counts[positions]
    lists = key_lists[positions]
    slot_ids = jnp.arange(span_table.shape[0], dtype=jnp.int32)
    slots = jnp.sum(
        jnp.where(lists[:, :, None] == span_table[None, None, :], slot_ids, 0), -1, dtype=jnp.int32
    )

    def by_head(x):
        x = x.reshape(local_blocks, BLOCK, GROUP, HEAD)
        stacked = jnp.transpose(x, (0, 2, 1, 3)).reshape(local_blocks, WIDE, HEAD)
        turned = jnp.transpose(x, (0, 3, 2, 1)).reshape(local_blocks, HEAD, WIDE)
        return stacked, turned

    qs, qt = by_head(queries)
    dos, dot = by_head(output_gradient)
    dqt, dkv = attend(counts, slots, qt, dot, qs, dos, kv_all)
    dq = jnp.transpose(dqt.reshape(local_blocks, HEAD, GROUP, BLOCK), (0, 3, 2, 1)) * SCALE
    grad_queries = dq.reshape(queries.shape).astype(BF16)

    seq_devices = lax.axis_size("seq")
    parts = lax.all_to_all(
        dkv.reshape(seq_devices, local_blocks * BLOCK, 2 * HEAD), "seq", split_axis=0, concat_axis=0
    )
    sums = jnp.sum(parts.astype(F32), 0)
    sums = jnp.concatenate([sums[:, :HEAD] * SCALE, sums[:, HEAD:]], 1).astype(BF16)
    mine = lax.all_to_all(
        sums.reshape(kv_devices, per_kvh, 2 * HEAD), "kvh", split_axis=0, concat_axis=0
    )
    mine = jnp.transpose(mine, (1, 0, 2)).reshape(per_kvh, kv_devices, 2, HEAD)
    key_gradient = mine[:, :, 0].reshape(per_kvh, kv_devices * HEAD)
    value_gradient = mine[:, :, 1].reshape(per_kvh, kv_devices * HEAD)
    return grad_queries, key_gradient, value_gradient


def solution(mesh):
    placed = (
        P("seq", "kvh"),
        P(("seq", "kvh"), None),
        P(("seq", "kvh"), None),
        P("seq", "kvh"),
        P(),
        P(),
        P(),
    )
    return jax.shard_map(
        shards,
        mesh=mesh,
        in_specs=placed,
        out_specs=(P("seq", "kvh"), P(("seq", "kvh"), None), P(("seq", "kvh"), None)),
        check_vma=False,
    )
```

```python
import functools

import jax
import jax.numpy as jnp
from jax import lax
from jax.experimental import pallas as pl
from jax.experimental.pallas import tpu as pltpu
from jax.sharding import PartitionSpec as P

HEAD = 128
GROUP = 8
BLOCK = 128
SCALE = HEAD ** (-0.5)
LOG2E = 1.4426950408889634
SCORE_SCALE = SCALE * LOG2E
TILE = 2 * BLOCK
WIDE = GROUP * BLOCK
BF16 = jnp.bfloat16
F32 = jnp.float32


def attend_kernel(groups, pieces, place, counts, slots, qt_ref, dot_ref, qs_ref, dos_ref, *refs):
    group_refs, refs = refs[:groups], refs[groups:]
    dqt_ref, refs = refs[0], refs[1:]
    out_refs, refs = refs[:groups], refs[groups:]
    kv_ref, kt_scr, total_scr, delta_scr, w_scr, ds_scr, acc_scr, sems = refs
    local_blocks = qt_ref.shape[0]
    n_slots = kv_ref.shape[0] // BLOCK
    span = kv_ref.shape[0] // groups
    part = span // pieces

    def rows_at(p, j):
        return pl.ds(pl.multiple_of(p * span + (place[0] ^ j) * part, part), part)

    copies = []
    for p in range(groups):
        for j in range(pieces):
            copies.append(
                pltpu.make_async_copy(
                    group_refs[p].at[pl.ds(j * part, part)], kv_ref.at[rows_at(p, j)], sems.at[p, j]
                )
            )
    for copy in copies:
        copy.start()
    acc_scr[...] = jnp.zeros_like(acc_scr)
    dqt_ref[...] = jnp.zeros_like(dqt_ref)
    total_scr[...] = jnp.zeros_like(total_scr)
    delta_scr[...] = jnp.zeros_like(delta_scr)

    for copy in copies:
        copy.wait()

    def turn(j, carry):
        rows = pl.ds(pl.multiple_of(j * BLOCK, BLOCK), BLOCK)
        kt_scr[j] = kv_ref[rows, :HEAD].T
        return carry

    lax.fori_loop(0, n_slots, turn, 0)

    def rows_of(i, entry):
        return pl.ds(pl.multiple_of(slots[i, entry] * BLOCK, BLOCK), BLOCK)

    def allowed(i, chunk):
        key_at = lax.broadcasted_iota(jnp.int32, (TILE, TILE), 0)
        query_at = lax.broadcasted_iota(jnp.int32, (TILE, TILE), 1) & (BLOCK - 1)
        second = key_at >= BLOCK
        entry = 2 * chunk + second.astype(jnp.int32)
        here = key_at & (BLOCK - 1)
        causal = jnp.logical_or(entry > 0, here <= query_at)
        return jnp.logical_and(entry < counts[i], causal)

    def pair(ref, i, chunk, lanes):
        return jnp.concatenate(
            [ref[rows_of(i, 2 * chunk), lanes], ref[rows_of(i, 2 * chunk + 1), lanes]], 0
        )

    def first_pass(i, chunk, masked):
        keys = pair(kv_ref, i, chunk, slice(0, HEAD))
        values = pair(kv_ref, i, chunk, slice(HEAD, 2 * HEAD))
        mask = allowed(i, chunk) if masked else None
        for h in range(0, WIDE, TILE):
            lanes = slice(h, h + TILE)
            scores = jnp.dot(keys, qt_ref[i, :, lanes], preferred_element_type=F32)
            expd = jnp.exp2(scores * SCORE_SCALE)
            if masked:
                expd = jnp.where(mask, expd, 0.0)
            total_scr[i, :, lanes] += jnp.sum(expd.reshape(TILE // 8, 8, TILE), 0)
            dweights = jnp.dot(values, dot_ref[i, :, lanes], preferred_element_type=F32)
            delta_scr[i, :, lanes] += jnp.sum((expd * dweights).reshape(TILE // 8, 8, TILE), 0)

    def second_pass(i, chunk, masked):
        keys = pair(kv_ref, i, chunk, slice(0, HEAD))
        values = pair(kv_ref, i, chunk, slice(HEAD, 2 * HEAD))
        mask = allowed(i, chunk) if masked else None
        keys_t = jnp.concatenate([kt_scr[slots[i, 2 * chunk]], kt_scr[slots[i, 2 * chunk + 1]]], 1)
        for h in range(0, WIDE, TILE):
            lanes = slice(h, h + TILE)
            scores = jnp.dot(keys, qt_ref[i, :, lanes], preferred_element_type=F32)
            weights = jnp.exp2(scores * SCORE_SCALE - total_scr[i, 0:1, lanes])
            if masked:
                weights = jnp.where(mask, weights, 0.0)
            dweights = jnp.dot(values, dot_ref[i, :, lanes], preferred_element_type=F32)
            dscores = (weights * (dweights - delta_scr[i, 0:1, lanes])).astype(BF16)
            w_scr[:, lanes] = weights.astype(BF16)
            ds_scr[:, lanes] = dscores
            dqt_ref[i, :, lanes] += jnp.dot(keys_t, dscores, preferred_element_type=F32)
        dk = jnp.dot(ds_scr[...], qs_ref[i], preferred_element_type=F32)
        dv = jnp.dot(w_scr[...], dos_ref[i], preferred_element_type=F32)
        for half in range(2):
            rows = rows_of(i, 2 * chunk + half)
            part = slice(half * BLOCK, (half + 1) * BLOCK)
            acc_scr[rows, :HEAD] += dk[part]
            acc_scr[rows, HEAD:] += dv[part]

    def sweep(i, step):
        chunks = (counts[i] + 1) // 2

        def body(chunk, carry):
            special = jnp.logical_or(chunk == 0, 2 * chunk + 2 > counts[i])

            @pl.when(special)
            def _():
                step(i, chunk, True)

            @pl.when(jnp.logical_not(special))
            def _():
                step(i, chunk, False)

            return carry

        lax.fori_loop(0, chunks, body, 0)

    def one_block(i, carry):
        sweep(i, first_pass)
        total = jnp.sum(total_scr[i], 0, keepdims=True)
        delta = jnp.sum(delta_scr[i], 0, keepdims=True) / total
        total_scr[i] = jnp.broadcast_to(jnp.log2(total), (8, WIDE))
        delta_scr[i] = jnp.broadcast_to(delta, (8, WIDE))
        sweep(i, second_pass)
        return carry

    lax.fori_loop(0, local_blocks, one_block, 0)
    for p in range(groups):
        for j in range(pieces):
            out_refs[p][j * part : (j + 1) * part] = acc_scr[rows_at(p, j)].astype(out_refs[p].dtype)


def attend(place, counts, slots, qt, dot, qs, dos, groups, pieces):
    local_blocks = qt.shape[0]
    rows = groups[0].shape[0] * len(groups)
    smem = pl.BlockSpec(memory_space=pltpu.SMEM)
    vmem = pl.BlockSpec(memory_space=pltpu.VMEM)
    return pl.pallas_call(
        functools.partial(attend_kernel, len(groups), pieces),
        in_specs=[smem] * 3 + [vmem] * 4 + [pl.BlockSpec(memory_space=pl.ANY)] * len(groups),
        out_specs=[vmem] * (1 + len(groups)),
        out_shape=[jax.ShapeDtypeStruct((local_blocks, HEAD, WIDE), F32)]
        + [jax.ShapeDtypeStruct(g.shape, BF16 if p & 1 else F32) for p, g in enumerate(groups)],
        scratch_shapes=[
            pltpu.VMEM((rows, 2 * HEAD), BF16),
            pltpu.VMEM((rows // BLOCK, HEAD, BLOCK), BF16),
            pltpu.VMEM((local_blocks, 8, WIDE), F32),
            pltpu.VMEM((local_blocks, 8, WIDE), F32),
            pltpu.VMEM((TILE, WIDE), BF16),
            pltpu.VMEM((TILE, WIDE), BF16),
            pltpu.VMEM((rows, 2 * HEAD), F32),
            pltpu.SemaphoreType.DMA((len(groups), pieces)),
        ],
        compiler_params=pltpu.CompilerParams(vmem_limit_bytes=48 << 20),
        name="attend",
    )(place, counts, slots, qt, dot, qs, dos, *groups)


def shards(
    queries,
    key_vector_rows,
    value_vector_rows,
    output_gradient,
    key_lists,
    block_counts,
    span_table,
):
    local_blocks = queries.shape[0] // BLOCK
    seq_devices, kv_devices = lax.axis_size("seq"), lax.axis_size("kvh")
    seq_at, kv_at = lax.axis_index("seq"), lax.axis_index("kvh")
    per_kvh = key_vector_rows.shape[0]

    def swap(x, seq_step, kv_step):
        if seq_step == 0 and kv_step == 0:
            return x
        pairs = [
            (s * kv_devices + h, (s ^ seq_step) * kv_devices + (h ^ kv_step))
            for s in range(seq_devices)
            for h in range(kv_devices)
        ]
        return lax.ppermute(x, ("seq", "kvh"), pairs)

    def head_rows(head):
        start = head * HEAD
        return jnp.concatenate(
            [
                lax.dynamic_slice_in_dim(key_vector_rows, start, HEAD, 1),
                lax.dynamic_slice_in_dim(value_vector_rows, start, HEAD, 1),
            ],
            1,
        )

    to_send = [head_rows(kv_at ^ j) for j in range(kv_devices)]
    far_first = range(seq_devices - 4, -1, -4)
    groups = [None] * seq_devices
    for far in far_first:
        groups[far] = jnp.concatenate(
            [swap(to_send[j], far, j) for j in range(kv_devices)], 0
        )
    for far in far_first:
        groups[far + 2] = swap(groups[far], 2, 0)
    for far in far_first:
        groups[far + 1] = swap(groups[far], 1, 0)
        groups[far + 3] = swap(groups[far + 2], 1, 0)

    first_slot = seq_at * local_blocks
    positions = lax.dynamic_slice_in_dim(span_table, first_slot, local_blocks, 0)
    counts = block_counts[positions]
    lists = key_lists[positions]
    slot_ids = jnp.arange(span_table.shape[0], dtype=jnp.int32) ^ first_slot
    slots = jnp.sum(
        jnp.where(lists[:, :, None] == span_table[None, None, :], slot_ids, 0), -1, dtype=jnp.int32
    )

    def by_head(x):
        x = x.reshape(local_blocks, BLOCK, GROUP, HEAD)
        stacked = jnp.transpose(x, (0, 2, 1, 3)).reshape(local_blocks, WIDE, HEAD)
        turned = jnp.transpose(x, (0, 3, 2, 1)).reshape(local_blocks, HEAD, WIDE)
        return stacked, turned

    qs, qt = by_head(queries)
    dos, dot = by_head(output_gradient)
    place = jnp.full((1,), kv_at, jnp.int32)
    dqt, *partials = attend(place, counts, slots, qt, dot, qs, dos, groups, kv_devices)
    dq = jnp.transpose(dqt.reshape(local_blocks, HEAD, GROUP, BLOCK), (0, 3, 2, 1)) * SCALE
    grad_queries = dq.reshape(queries.shape).astype(BF16)

    sums = [0.0] * kv_devices
    for far in far_first:
        near = [partials[far + y] + swap(partials[far + y + 1], 1, 0).astype(F32) for y in (0, 2)]
        other = swap(near[1].astype(BF16), 2, 0)
        chip = (near[0] + other.astype(F32)).astype(BF16)
        for j in range(kv_devices):
            got = swap(chip[j * per_kvh : (j + 1) * per_kvh], far, j)
            sums[j] = sums[j] + got.astype(F32)
    stacked = jnp.stack(sums)
    heads = [lax.dynamic_index_in_dim(stacked, kv_at ^ j, 0, False) for j in range(kv_devices)]
    key_gradient = jnp.concatenate([x[:, :HEAD] * SCALE for x in heads], 1).astype(BF16)
    value_gradient = jnp.concatenate([x[:, HEAD:] for x in heads], 1).astype(BF16)
    return grad_queries, key_gradient, value_gradient


def solution(mesh):
    placed = (
        P("seq", "kvh"),
        P(("seq", "kvh"), None),
        P(("seq", "kvh"), None),
        P("seq", "kvh"),
        P(),
        P(),
        P(),
    )
    return jax.shard_map(
        shards,
        mesh=mesh,
        in_specs=placed,
        out_specs=(P("seq", "kvh"), P(("seq", "kvh"), None), P(("seq", "kvh"), None)),
        check_vma=False,
    )
```

```python
import functools

import jax
import jax.numpy as jnp
from jax import lax
from jax.experimental import pallas as pl
from jax.experimental.pallas import tpu as pltpu
from jax.sharding import PartitionSpec as P

HEAD = 128
GROUP = 8
BLOCK = 128
SCALE = HEAD ** (-0.5)
LOG2E = 1.4426950408889634
SCORE_SCALE = SCALE * LOG2E
TILE = 2 * BLOCK
WIDE = GROUP * BLOCK
BF16 = jnp.bfloat16
F32 = jnp.float32


def attend_kernel(counts, slots, qt_ref, dot_ref, qs_ref, dos_ref, *refs):
    part_refs, (dqt_ref, *out_refs), scratch = refs[:4], refs[4:9], refs[9:]
    kv_ref, total_scr, delta_scr, w_scr, ds_scr, acc_scr, sems = scratch
    local_blocks = qt_ref.shape[0]
    part_rows = kv_ref.shape[0] // 4

    def part_of(p):
        return slice(p * part_rows, (p + 1) * part_rows)

    copies = [
        pltpu.make_async_copy(part_refs[p], kv_ref.at[part_of(p)], sems.at[p]) for p in range(4)
    ]
    for copy in copies:
        copy.start()
    acc_scr[...] = jnp.zeros_like(acc_scr)
    dqt_ref[...] = jnp.zeros_like(dqt_ref)
    total_scr[...] = jnp.zeros_like(total_scr)
    delta_scr[...] = jnp.zeros_like(delta_scr)

    for copy in copies:
        copy.wait()

    def rows_of(i, entry):
        return pl.ds(pl.multiple_of(slots[i, entry] * BLOCK, BLOCK), BLOCK)

    def allowed(i, chunk):
        key_at = lax.broadcasted_iota(jnp.int32, (TILE, TILE), 0)
        query_at = lax.broadcasted_iota(jnp.int32, (TILE, TILE), 1) & (BLOCK - 1)
        second = key_at >= BLOCK
        entry = 2 * chunk + second.astype(jnp.int32)
        here = key_at & (BLOCK - 1)
        causal = jnp.logical_or(entry > 0, here <= query_at)
        return jnp.logical_and(entry < counts[i], causal)

    def pair(ref, i, chunk, lanes):
        return jnp.concatenate(
            [ref[rows_of(i, 2 * chunk), lanes], ref[rows_of(i, 2 * chunk + 1), lanes]], 0
        )

    def first_pass(i, chunk, masked):
        keys = pair(kv_ref, i, chunk, slice(0, HEAD))
        values = pair(kv_ref, i, chunk, slice(HEAD, 2 * HEAD))
        mask = allowed(i, chunk) if masked else None
        for h in range(0, WIDE, TILE):
            lanes = slice(h, h + TILE)
            scores = jnp.dot(keys, qt_ref[i, :, lanes], preferred_element_type=F32)
            expd = jnp.exp2(scores * SCORE_SCALE)
            if masked:
                expd = jnp.where(mask, expd, 0.0)
            total_scr[i, :, lanes] += jnp.sum(expd.reshape(TILE // 8, 8, TILE), 0)
            dweights = jnp.dot(values, dot_ref[i, :, lanes], preferred_element_type=F32)
            delta_scr[i, :, lanes] += jnp.sum((expd * dweights).reshape(TILE // 8, 8, TILE), 0)

    def second_pass(i, chunk, masked):
        keys = pair(kv_ref, i, chunk, slice(0, HEAD))
        values = pair(kv_ref, i, chunk, slice(HEAD, 2 * HEAD))
        mask = allowed(i, chunk) if masked else None
        for h in range(0, WIDE, TILE):
            lanes = slice(h, h + TILE)
            scores = jnp.dot(keys, qt_ref[i, :, lanes], preferred_element_type=F32)
            weights = jnp.exp2(scores * SCORE_SCALE - total_scr[i, 0:1, lanes])
            if masked:
                weights = jnp.where(mask, weights, 0.0)
            dweights = jnp.dot(values, dot_ref[i, :, lanes], preferred_element_type=F32)
            dscores = (weights * (dweights - delta_scr[i, 0:1, lanes])).astype(BF16)
            w_scr[:, lanes] = weights.astype(BF16)
            ds_scr[:, lanes] = dscores
        dqt_ref[i] += jnp.dot(keys.T, ds_scr[...], preferred_element_type=F32)
        dk = jnp.dot(ds_scr[...], qs_ref[i], preferred_element_type=F32)
        dv = jnp.dot(w_scr[...], dos_ref[i], preferred_element_type=F32)
        for half in range(2):
            rows = rows_of(i, 2 * chunk + half)
            part = slice(half * BLOCK, (half + 1) * BLOCK)
            acc_scr[rows, :HEAD] += dk[part]
            acc_scr[rows, HEAD:] += dv[part]

    def sweep(i, step):
        chunks = (counts[i] + 1) // 2

        def body(chunk, carry):
            special = jnp.logical_or(chunk == 0, 2 * chunk + 2 > counts[i])

            @pl.when(special)
            def _():
                step(i, chunk, True)

            @pl.when(jnp.logical_not(special))
            def _():
                step(i, chunk, False)

            return carry

        lax.fori_loop(0, chunks, body, 0)

    def one_block(i, carry):
        sweep(i, first_pass)
        total = jnp.sum(total_scr[i], 0, keepdims=True)
        delta = jnp.sum(delta_scr[i], 0, keepdims=True) / total
        total_scr[i] = jnp.broadcast_to(jnp.log2(total), (8, WIDE))
        delta_scr[i] = jnp.broadcast_to(delta, (8, WIDE))
        sweep(i, second_pass)
        return carry

    lax.fori_loop(0, local_blocks, one_block, 0)
    for p in range(4):
        out_refs[p][...] = acc_scr[part_of(p)].astype(out_refs[p].dtype)


def attend(counts, slots, qt, dot, qs, dos, parts):
    local_blocks = qt.shape[0]
    rows = 4 * parts[0].shape[0]
    smem = pl.BlockSpec(memory_space=pltpu.SMEM)
    vmem = pl.BlockSpec(memory_space=pltpu.VMEM)
    return pl.pallas_call(
        attend_kernel,
        in_specs=[smem] * 2 + [vmem] * 4 + [pl.BlockSpec(memory_space=pl.ANY)] * 4,
        out_specs=[vmem] * 5,
        out_shape=[jax.ShapeDtypeStruct((local_blocks, HEAD, WIDE), F32)]
        + [jax.ShapeDtypeStruct(x.shape, BF16 if p & 1 else F32) for p, x in enumerate(parts)],
        scratch_shapes=[
            pltpu.VMEM((rows, 2 * HEAD), BF16),
            pltpu.VMEM((local_blocks, 8, WIDE), F32),
            pltpu.VMEM((local_blocks, 8, WIDE), F32),
            pltpu.VMEM((TILE, WIDE), BF16),
            pltpu.VMEM((TILE, WIDE), BF16),
            pltpu.VMEM((rows, 2 * HEAD), F32),
            pltpu.SemaphoreType.DMA((4,)),
        ],
        compiler_params=pltpu.CompilerParams(vmem_limit_bytes=(16 << 20) + rows * 4096),
        name="attend",
    )(counts, slots, qt, dot, qs, dos, *parts)


def shards(
    queries,
    key_vector_rows,
    value_vector_rows,
    output_gradient,
    key_lists,
    block_counts,
    span_table,
):
    local_blocks = queries.shape[0] // BLOCK
    seq_devices, kv_devices = lax.axis_size("seq"), lax.axis_size("kvh")
    seq_at = lax.axis_index("seq")
    per_kvh = key_vector_rows.shape[0]
    half, middles = seq_devices // 2, seq_devices // 4
    near_devices = middles * kv_devices
    near_groups = [
        [
            (top * half + middle * 2 + core) * kv_devices + head
            for middle in range(middles)
            for head in range(kv_devices)
        ]
        for top in range(2)
        for core in range(2)
    ]

    def swap_core(x):
        return lax.ppermute(x, "seq", [(s, s ^ 1) for s in range(seq_devices)])

    def swap_far(x):
        return lax.ppermute(x, "seq", [(s, s ^ half) for s in range(seq_devices)])

    def exchange_near(x):
        return lax.all_to_all(x, ("seq", "kvh"), 0, 0, axis_index_groups=near_groups)

    def by_kv_head(x):
        return jnp.transpose(x.reshape(per_kvh, kv_devices, HEAD), (1, 0, 2))

    def to_all_near(x):
        x = jnp.broadcast_to(x[None], (middles, *x.shape))
        x = exchange_near(x.reshape(near_devices, per_kvh, 2 * HEAD))
        return x.reshape(near_devices * per_kvh, 2 * HEAD)

    own = jnp.concatenate([by_kv_head(key_vector_rows), by_kv_head(value_vector_rows)], 2)
    far = swap_far(own)
    near_part = to_all_near(own)
    far_part = to_all_near(far)
    parts = [near_part, swap_core(near_part), far_part, swap_core(far_part)]

    first_slot = seq_at * local_blocks
    positions = lax.dynamic_slice_in_dim(span_table, first_slot, local_blocks, 0)
    counts = block_counts[positions]
    lists = key_lists[positions]
    slot_ids = jnp.arange(span_table.shape[0], dtype=jnp.int32)
    owner = slot_ids // local_blocks
    part = (owner // half ^ seq_at // half) * 2 + (owner % 2 ^ seq_at % 2)
    place = (part * middles + owner % half // 2) * local_blocks + slot_ids % local_blocks
    slots = jnp.sum(
        jnp.where(lists[:, :, None] == span_table[None, None, :], place, 0), -1, dtype=jnp.int32
    )

    def by_head(x):
        x = x.reshape(local_blocks, BLOCK, GROUP, HEAD)
        stacked = jnp.transpose(x, (0, 2, 1, 3)).reshape(local_blocks, WIDE, HEAD)
        turned = jnp.transpose(x, (0, 3, 2, 1)).reshape(local_blocks, HEAD, WIDE)
        return stacked, turned

    qs, qt = by_head(queries)
    dos, dot = by_head(output_gradient)
    dqt, *partials = attend(counts, slots, qt, dot, qs, dos, parts)
    dq = jnp.transpose(dqt.reshape(local_blocks, HEAD, GROUP, BLOCK), (0, 3, 2, 1)) * SCALE
    grad_queries = dq.reshape(queries.shape).astype(BF16)

    def near_sums(kept, sent):
        chip = (kept + swap_core(sent).astype(F32)).astype(BF16)
        got = exchange_near(chip.reshape(near_devices, per_kvh, 2 * HEAD))
        return jnp.sum(got.reshape(middles, kv_devices, per_kvh, 2 * HEAD).astype(F32), 0)

    far_sums = swap_far(near_sums(partials[2], partials[3]).astype(BF16))
    sums = near_sums(partials[0], partials[1]) + far_sums.astype(F32)

    def by_token(x):
        return jnp.transpose(x, (1, 0, 2)).reshape(per_kvh, kv_devices * HEAD).astype(BF16)

    return grad_queries, by_token(sums[:, :, :HEAD] * SCALE), by_token(sums[:, :, HEAD:])


def solution(mesh):
    placed = (
        P("seq", "kvh"),
        P(("seq", "kvh"), None),
        P(("seq", "kvh"), None),
        P("seq", "kvh"),
        P(),
        P(),
        P(),
    )
    return jax.shard_map(
        shards,
        mesh=mesh,
        in_specs=placed,
        out_specs=(P("seq", "kvh"), P(("seq", "kvh"), None), P(("seq", "kvh"), None)),
        check_vma=False,
    )
```

```python
import functools

import jax
import jax.numpy as jnp
from jax import lax
from jax.experimental import pallas as pl
from jax.experimental.pallas import tpu as pltpu
from jax.sharding import PartitionSpec as P

HEAD = 128
GROUP = 8
BLOCK = 128
SCALE = HEAD ** (-0.5)
LOG2E = 1.4426950408889634
SCORE_SCALE = SCALE * LOG2E
TILE = 2 * BLOCK
WIDE = GROUP * BLOCK
BF16 = jnp.bfloat16
F32 = jnp.float32
BY_ROWS = (((1,), (1,)), ((), ()))


def by_rows(a, b):
    return lax.dot_general(a, b, BY_ROWS, preferred_element_type=F32)


def plain(a, b):
    return jnp.dot(a, b, preferred_element_type=F32)


def start_copies(sources, targets, sems):
    copies = [pltpu.make_async_copy(a, b, sems.at[n]) for n, (a, b) in enumerate(zip(sources, targets))]
    for copy in copies:
        copy.start()
    return copies


def find_places(me, spans, place, local_blocks):
    n_slots = spans.shape[0]
    half, middles = n_slots // local_blocks // 2, n_slots // local_blocks // 4
    seq_at, turn = me[0], me[1]

    def find(slot, carry):
        owner, block = slot // local_blocks, slot % local_blocks
        apart = owner ^ seq_at
        is_far = apart // half
        near_at = apart % half // 2 * local_blocks + (block ^ turn // BLOCK)
        far_at = owner % half // 2 * local_blocks + block
        part = is_far * 2 + apart % 2
        place[spans[slot]] = part * (middles * local_blocks) + jnp.where(is_far == 1, far_at, near_at)
        return carry

    lax.fori_loop(0, n_slots, find, 0)


def choose(me, lists, counts, spans, place, work, sizes, local_blocks, want_far):
    n_slots = spans.shape[0]
    for i in range(local_blocks):
        at = spans[me[0] * local_blocks + i]

        def clear(e, carry):
            work[i, e] = 0
            return carry

        def keep(e, size):
            here = place[lists[at, e]]
            work[i, size] = here
            return size + (here // (n_slots // 2) == want_far).astype(jnp.int32)

        lax.fori_loop(0, work.shape[1], clear, 0)
        size = lax.fori_loop(0, counts[at], keep, 0)
        work[i, size] = 0
        sizes[i] = size


def heads(ref, i, first, many):
    rows = pl.ds(pl.multiple_of(i * BLOCK, BLOCK), BLOCK)
    return jnp.concatenate([ref[rows, h * HEAD : (h + 1) * HEAD] for h in range(first, first + many)], 0)


def rows_at(place):
    return pl.ds(pl.multiple_of(place * BLOCK, BLOCK), BLOCK)


def gathered(kv_ref, places, lanes):
    return jnp.concatenate([kv_ref[rows_at(p), lanes] for p in places], 0)


def allowed(many, start, count, turn, diagonal):
    key_at = lax.broadcasted_iota(jnp.int32, (many * BLOCK, TILE), 0)
    entry = start + key_at // BLOCK
    mask = entry < count
    if diagonal:
        query_at = lax.broadcasted_iota(jnp.int32, (many * BLOCK, TILE), 1) & (BLOCK - 1)
        here = (key_at & (BLOCK - 1)) ^ (turn & (BLOCK - 1))
        mask = jnp.logical_and(mask, jnp.logical_or(entry > 0, here <= query_at))
    return mask


def sweep(count, step):
    rest = count % 4
    quads = count // 4 + (rest == 3).astype(jnp.int32)

    def body(quad, carry):
        special = jnp.logical_or(quad == 0, 4 * quad + 4 > count)

        @pl.when(special)
        def _():
            step(4 * quad, 4, True)

        @pl.when(jnp.logical_not(special))
        def _():
            step(4 * quad, 4, False)

        return carry

    lax.fori_loop(0, quads, body, 0)

    @pl.when(jnp.logical_or(rest == 1, rest == 2))
    def _():
        step(4 * quads, 2, True)


def first_pass(i, places, mask, q_ref, do_ref, kv_ref, total, delta):
    keys = gathered(kv_ref, places, slice(0, HEAD))
    values = gathered(kv_ref, places, slice(HEAD, 2 * HEAD))
    for h in range(0, GROUP, 2):
        lanes = slice(h * BLOCK, h * BLOCK + TILE)
        expd = jnp.exp2(by_rows(keys, heads(q_ref, i, h, 2)) * SCORE_SCALE)
        if mask is not None:
            expd = jnp.where(mask, expd, 0.0)
        total[i, :, lanes] += jnp.sum(expd.reshape(-1, 8, TILE), 0)
        dweights = by_rows(values, heads(do_ref, i, h, 2))
        delta[i, :, lanes] += jnp.sum((expd * dweights).reshape(-1, 8, TILE), 0)


def near_kernel(me, lists, counts, spans, q_any, do_any, near_any, pair_any, total, delta, *scratch):
    q_ref, do_ref, kv_ref, place, work, sizes, sems = scratch
    local_blocks, part = q_ref.shape[0] // BLOCK, near_any.shape[0]
    copies = start_copies(
        [near_any, pair_any, q_any, do_any],
        [kv_ref.at[:part], kv_ref.at[part:], q_ref, do_ref],
        sems,
    )
    total[...] = jnp.zeros_like(total)
    delta[...] = jnp.zeros_like(delta)
    find_places(me, spans, place, local_blocks)
    choose(me, lists, counts, spans, place, work, sizes, local_blocks, 0)
    for copy in copies:
        copy.wait()

    def one_block(i, carry):
        def step(start, many, masked):
            mask = allowed(many, start, sizes[i], me[1], True) if masked else None
            places = [work[i, start + e] for e in range(many)]
            first_pass(i, places, mask, q_ref, do_ref, kv_ref, total, delta)

        sweep(sizes[i], step)
        return carry

    lax.fori_loop(0, local_blocks, one_block, 0)


def main_kernel(me, lists, counts, spans, q_any, do_any, total_in, delta_in, *refs):
    part_refs, (dqt_ref, *out_refs), scratch = refs[:4], refs[4:9], refs[9:]
    q_ref, do_ref, kv_ref, total, delta, w_scr, ds_scr, acc, place, work, sizes, sems = scratch
    local_blocks, part = q_ref.shape[0] // BLOCK, part_refs[0].shape[0]

    def part_of(p):
        return slice(p * part, (p + 1) * part)

    copies = start_copies(
        [*part_refs, q_any, do_any], [*(kv_ref.at[part_of(p)] for p in range(4)), q_ref, do_ref], sems
    )
    acc[...] = jnp.zeros_like(acc)
    dqt_ref[...] = jnp.zeros_like(dqt_ref)
    total[...] = total_in[...]
    delta[...] = delta_in[...]
    find_places(me, spans, place, local_blocks)
    choose(me, lists, counts, spans, place, work, sizes, local_blocks, 1)
    for copy in copies:
        copy.wait()

    def second_pass(i, places, mask):
        keys = gathered(kv_ref, places, slice(0, HEAD))
        values = gathered(kv_ref, places, slice(HEAD, 2 * HEAD))
        rows = slice(0, len(places) * BLOCK)
        for h in range(0, GROUP, 2):
            lanes = slice(h * BLOCK, h * BLOCK + TILE)
            scores = by_rows(keys, heads(q_ref, i, h, 2))
            weights = jnp.exp2(scores * SCORE_SCALE - total[i, 0:1, lanes])
            if mask is not None:
                weights = jnp.where(mask, weights, 0.0)
            dweights = by_rows(values, heads(do_ref, i, h, 2))
            w_scr[rows, lanes] = weights.astype(BF16)
            ds_scr[rows, lanes] = (weights * (dweights - delta[i, 0:1, lanes])).astype(BF16)
        dqt_ref[i] += plain(keys.T, ds_scr[rows])
        dk = plain(ds_scr[rows], heads(q_ref, i, 0, GROUP))
        dv = plain(w_scr[rows], heads(do_ref, i, 0, GROUP))
        for n, p in enumerate(places):
            acc[rows_at(p), :HEAD] += dk[n * BLOCK : (n + 1) * BLOCK]
            acc[rows_at(p), HEAD:] += dv[n * BLOCK : (n + 1) * BLOCK]

    def one_block(i, carry):
        at = spans[me[0] * local_blocks + i]
        count = counts[at]

        def far_step(start, many, masked):
            mask = allowed(many, start, sizes[i], me[1], False) if masked else None
            places = [work[i, start + e] for e in range(many)]
            first_pass(i, places, mask, q_ref, do_ref, kv_ref, total, delta)

        def step(start, many, masked):
            mask = allowed(many, start, count, me[1], True) if masked else None
            second_pass(i, [place[lists[at, start + e]] for e in range(many)], mask)

        sweep(sizes[i], far_step)
        row_total = jnp.sum(total[i], 0, keepdims=True)
        row_delta = jnp.sum(delta[i], 0, keepdims=True) / row_total
        total[i] = jnp.broadcast_to(jnp.log2(row_total), (8, WIDE))
        delta[i] = jnp.broadcast_to(row_delta, (8, WIDE))
        sweep(count, step)
        return carry

    lax.fori_loop(0, local_blocks, one_block, 0)
    for p in range(4):
        out_refs[p][...] = acc[part_of(p)].astype(out_refs[p].dtype)


LIMIT = 32 << 20
SMEM = pl.BlockSpec(memory_space=pltpu.SMEM)
VMEM = pl.BlockSpec(memory_space=pltpu.VMEM)
ANY = pl.BlockSpec(memory_space=pl.ANY)


def lists_scratch(lists, spans, local_blocks):
    return [
        pltpu.SMEM(spans.shape, jnp.int32),
        pltpu.SMEM((local_blocks, lists.shape[1] + 8), jnp.int32),
        pltpu.SMEM((local_blocks,), jnp.int32),
    ]


def near_sums(me, lists, counts, spans, q, do, near, pair):
    local_blocks, rows = q.shape[0] // BLOCK, 2 * near.shape[0]
    return pl.pallas_call(
        near_kernel,
        in_specs=[SMEM] * 4 + [ANY] * 4,
        out_specs=[VMEM] * 2,
        out_shape=[jax.ShapeDtypeStruct((local_blocks, 8, WIDE), F32)] * 2,
        scratch_shapes=[
            pltpu.VMEM(q.shape, BF16),
            pltpu.VMEM(do.shape, BF16),
            pltpu.VMEM((rows, 2 * HEAD), BF16),
            *lists_scratch(lists, spans, local_blocks),
            pltpu.SemaphoreType.DMA((4,)),
        ],
        compiler_params=pltpu.CompilerParams(vmem_limit_bytes=LIMIT),
        cost_estimate=pl.CostEstimate(flops=1 << 20, bytes_accessed=1 << 10, transcendentals=0),
        name="near",
    )(me, lists, counts, spans, q, do, near, pair)


def attend(me, lists, counts, spans, q, do, total, delta, parts):
    local_blocks, rows = q.shape[0] // BLOCK, 4 * parts[0].shape[0]
    return pl.pallas_call(
        main_kernel,
        in_specs=[SMEM] * 4 + [ANY] * 2 + [VMEM] * 2 + [ANY] * 4,
        out_specs=[VMEM] * 5,
        out_shape=[jax.ShapeDtypeStruct((local_blocks, HEAD, WIDE), F32)]
        + [jax.ShapeDtypeStruct(x.shape, BF16 if p & 1 else F32) for p, x in enumerate(parts)],
        scratch_shapes=[
            pltpu.VMEM(q.shape, BF16),
            pltpu.VMEM(do.shape, BF16),
            pltpu.VMEM((rows, 2 * HEAD), BF16),
            pltpu.VMEM((local_blocks, 8, WIDE), F32),
            pltpu.VMEM((local_blocks, 8, WIDE), F32),
            pltpu.VMEM((4 * BLOCK, WIDE), BF16),
            pltpu.VMEM((4 * BLOCK, WIDE), BF16),
            pltpu.VMEM((rows, 2 * HEAD), F32),
            *lists_scratch(lists, spans, local_blocks),
            pltpu.SemaphoreType.DMA((6,)),
        ],
        compiler_params=pltpu.CompilerParams(vmem_limit_bytes=LIMIT),
        name="attend",
    )(me, lists, counts, spans, q, do, total, delta, *parts)


def shards(
    queries,
    key_vector_rows,
    value_vector_rows,
    output_gradient,
    key_lists,
    block_counts,
    span_table,
):
    seq_devices, kv_devices = lax.axis_size("seq"), lax.axis_size("kvh")
    seq_at, kv_at = lax.axis_index("seq"), lax.axis_index("kvh")
    per_kvh = key_vector_rows.shape[0]
    half, middles = seq_devices // 2, seq_devices // 4
    near_devices = middles * kv_devices
    near_groups = [
        [
            (top * half + middle * 2 + core) * kv_devices + head
            for middle in range(middles)
            for head in range(kv_devices)
        ]
        for top in range(2)
        for core in range(2)
    ]

    def swap_seq(x, step):
        return lax.ppermute(x, "seq", [(s, s ^ step) for s in range(seq_devices)])

    def swap_kv(x, step):
        return lax.ppermute(x, "kvh", [(h, h ^ step) for h in range(kv_devices)])

    def exchange_near(x):
        x = x.reshape(near_devices, per_kvh, 2 * HEAD)
        return lax.all_to_all(x, ("seq", "kvh"), 0, 0, axis_index_groups=near_groups)

    own = jnp.stack(
        [
            jnp.concatenate([x[:, h * HEAD : (h + 1) * HEAD] for x in (key_vector_rows, value_vector_rows)], 1)
            for h in range(kv_devices)
        ]
    )
    far = swap_seq(own, half)
    mine = [lax.dynamic_index_in_dim(own, kv_at ^ j, 0, False) for j in range(kv_devices)]
    span = jnp.concatenate([mine[0]] + [swap_kv(mine[j], j) for j in range(1, kv_devices)], 0)
    near_part = jnp.concatenate([span] + [swap_seq(span, 2 * m) for m in range(1, middles)], 0)
    near_pair = swap_seq(near_part, 1)
    far_part = exchange_near(jnp.broadcast_to(far[None], (middles, *far.shape)))
    far_part = far_part.reshape(near_part.shape)

    me = jnp.stack([seq_at, kv_at * per_kvh]).astype(jnp.int32)
    common = (me, key_lists, block_counts, span_table, queries, output_gradient)
    total, delta = near_sums(*common, near_part, near_pair)
    total, far_part = lax.optimization_barrier((total, far_part))
    far_pair = swap_seq(far_part, 1)
    dqt, *partials = attend(*common, total, delta, [near_part, near_pair, far_part, far_pair])
    dq = jnp.transpose(dqt.reshape(-1, HEAD, GROUP, BLOCK), (0, 3, 2, 1)) * SCALE
    grad_queries = dq.reshape(queries.shape).astype(BF16)

    far_chip = (partials[2] + swap_seq(partials[3], 1).astype(F32)).astype(BF16)
    far_sums = exchange_near(far_chip).reshape(middles, kv_devices, per_kvh, 2 * HEAD)
    far_sums = jnp.sum(far_sums.astype(F32), 0).astype(BF16)

    near_recv = swap_seq(partials[1], 1)
    span_rows = kv_devices * per_kvh

    def near_chip(m):
        rows = slice(m * span_rows, (m + 1) * span_rows)
        return partials[0][rows] + near_recv[rows].astype(F32)

    others = [swap_seq(near_chip(m).astype(BF16), 2 * m) for m in range(1, middles)]
    *others, _ = lax.optimization_barrier((*others, far_sums))
    far_sums = swap_seq(far_sums, half).astype(F32)
    span_sums = near_chip(0)
    for other in others:
        span_sums = span_sums + other.astype(F32)
    pieces = [span_sums[j * per_kvh : (j + 1) * per_kvh] for j in range(kv_devices)]
    pieces = pieces[:1] + [swap_kv(pieces[j].astype(BF16), j).astype(F32) for j in range(1, kv_devices)]
    pieces = jnp.stack(pieces)
    sums = [
        lax.dynamic_index_in_dim(pieces, kv_at ^ h, 0, False) + far_sums[h] for h in range(kv_devices)
    ]
    key_gradient = jnp.concatenate([x[:, :HEAD] * SCALE for x in sums], 1).astype(BF16)
    value_gradient = jnp.concatenate([x[:, HEAD:] for x in sums], 1).astype(BF16)
    return grad_queries, key_gradient, value_gradient


def solution(mesh):
    placed = (
        P("seq", "kvh"),
        P(("seq", "kvh"), None),
        P(("seq", "kvh"), None),
        P("seq", "kvh"),
        P(),
        P(),
        P(),
    )
    return jax.shard_map(
        shards,
        mesh=mesh,
        in_specs=placed,
        out_specs=(P("seq", "kvh"), P(("seq", "kvh"), None), P(("seq", "kvh"), None)),
        check_vma=False,
    )
```

```python
import functools

import jax
import jax.numpy as jnp
from jax import lax
from jax.experimental import pallas as pl
from jax.experimental.pallas import tpu as pltpu
from jax.sharding import PartitionSpec as P

HEAD = 128
GROUP = 8
BLOCK = 128
SCALE = HEAD ** (-0.5)
LOG2E = 1.4426950408889634
SCORE_SCALE = SCALE * LOG2E
TILE = 2 * BLOCK
WIDE = GROUP * BLOCK
BF16 = jnp.bfloat16
F32 = jnp.float32
BY_ROWS = (((1,), (1,)), ((), ()))


def by_rows(a, b):
    return lax.dot_general(a, b, BY_ROWS, preferred_element_type=F32)


def plain(a, b):
    return jnp.dot(a, b, preferred_element_type=F32)


def start_copies(sources, targets, sems):
    copies = [pltpu.make_async_copy(a, b, sems.at[n]) for n, (a, b) in enumerate(zip(sources, targets))]
    for copy in copies:
        copy.start()
    return copies


def here(part):
    return lax.axis_index("seq"), lax.axis_index("kvh") * part


def lists_kernel(part, lists, counts, spans, work, place):
    n_slots, local_blocks = spans.shape[0], (work.shape[0] - 1) // 3
    seq_at, turn = here(part)
    seq_bits = (n_slots // local_blocks).bit_length() - 1
    block_bits, half_bit = local_blocks.bit_length() - 1, seq_bits - 1
    part_bits = half_bit - 1 + block_bits

    def find(slot, carry):
        owner, block = slot >> block_bits, slot & (local_blocks - 1)
        apart = owner ^ seq_at
        is_far = apart >> half_bit
        middle = (jnp.where(is_far == 1, owner, apart) >> 1) & ((1 << (half_bit - 1)) - 1)
        block = jnp.where(is_far == 1, block, block ^ (turn >> 7))
        place[spans[slot]] = (((is_far << 1) | (apart & 1)) << part_bits) | (middle << block_bits) | block
        return carry

    lax.fori_loop(0, n_slots, find, 0, unroll=8)
    for i in range(local_blocks):
        at = spans[seq_at * local_blocks + i]
        near, far, every = (kind * local_blocks + i for kind in range(3))

        def clear(e, carry):
            for row in (near, far, every):
                work[row, e] = 0
            return carry

        def keep(e, sizes):
            found = place[lists[e, at]]
            is_far = found >> (part_bits + 1)
            work[near, sizes[0]] = found
            work[far, sizes[1]] = found
            work[every, e] = found
            return sizes[0] + 1 - is_far, sizes[1] + is_far

        lax.fori_loop(0, work.shape[1], clear, 0, unroll=8)
        near_size, far_size = lax.fori_loop(0, counts[at], keep, (0, 0))
        work[near, near_size] = 0
        work[far, far_size] = 0
        for kind, size in enumerate((near_size, far_size, counts[at])):
            work[3 * local_blocks, kind * local_blocks + i] = size


def heads(ref, i, first, many):
    rows = pl.ds(pl.multiple_of(i * BLOCK, BLOCK), BLOCK)
    return jnp.concatenate([ref[rows, h * HEAD : (h + 1) * HEAD] for h in range(first, first + many)], 0)


def rows_at(place):
    return pl.ds(pl.multiple_of(place * BLOCK, BLOCK), BLOCK)


def gathered(kv_ref, places, lanes):
    return jnp.concatenate([kv_ref[rows_at(p), lanes] for p in places], 0)


def allowed(many, count, turn, diagonal):
    if count is None:
        return None
    key_at = lax.broadcasted_iota(jnp.int32, (many * BLOCK, TILE), 0)
    entry = key_at // BLOCK
    mask = entry < count
    if diagonal:
        query_at = lax.broadcasted_iota(jnp.int32, (many * BLOCK, TILE), 1) & (BLOCK - 1)
        here = (key_at & (BLOCK - 1)) ^ (turn & (BLOCK - 1))
        mask = jnp.logical_and(mask, jnp.logical_or(entry > 0, here <= query_at))
    return mask


def split(count):
    first = (count + 3) % 4 + 1
    return first, (count - first) // 4


def sweep(count, step):
    first, quads = split(count)

    @pl.when(jnp.logical_and(count > 0, first <= 2))
    def _():
        step(0, 2, first)

    @pl.when(jnp.logical_and(count > 0, first > 2))
    def _():
        step(0, 4, first)

    def body(n, carry):
        step(first + 8 * n, 8, None)
        return carry

    lax.fori_loop(0, quads // 2, body, 0)

    @pl.when(jnp.logical_and(count > 0, quads % 2 == 1))
    def _():
        step(first + 4 * (quads - 1), 4, None)


def first_pass(i, places, mask, q_ref, do_ref, kv_ref, total, delta):
    keys = gathered(kv_ref, places, slice(0, HEAD))
    values = gathered(kv_ref, places, slice(HEAD, 2 * HEAD))
    for h in range(0, GROUP, 2):
        lanes = slice(h * BLOCK, h * BLOCK + TILE)
        expd = jnp.exp2(by_rows(keys, heads(q_ref, i, h, 2)) * SCORE_SCALE)
        if mask is not None:
            expd = jnp.where(mask, expd, 0.0)
        total[i, :, lanes] += jnp.sum(expd.reshape(-1, 8, TILE), 0)
        dweights = by_rows(values, heads(do_ref, i, h, 2))
        delta[i, :, lanes] += jnp.sum((expd * dweights).reshape(-1, 8, TILE), 0)


def near_kernel(part_rows, work, q_any, do_any, near_any, pair_any, total, delta, *scratch):
    q_ref, do_ref, kv_ref, sems = scratch
    local_blocks, part = q_ref.shape[0] // BLOCK, near_any.shape[0]
    _, turn = here(part_rows)
    copies = start_copies(
        [near_any, pair_any, q_any, do_any],
        [kv_ref.at[:part], kv_ref.at[part:], q_ref, do_ref],
        sems,
    )
    total[...] = jnp.zeros_like(total)
    delta[...] = jnp.zeros_like(delta)
    for copy in copies:
        copy.wait()

    def one_block(i, carry):
        def step(start, many, used):
            mask = allowed(many, used, turn, True)
            places = [work[i, start + e] for e in range(many)]
            first_pass(i, places, mask, q_ref, do_ref, kv_ref, total, delta)

        sweep(work[3 * local_blocks, i], step)
        return carry

    lax.fori_loop(0, local_blocks, one_block, 0)


def main_kernel(part_rows, work, q_any, do_any, total_in, delta_in, *refs):
    part_refs, (dqt_ref, *out_refs), scratch = refs[:4], refs[4:9], refs[9:]
    q_ref, do_ref, kv_ref, total, delta, w_scr, ds_scr, acc, sems = scratch
    local_blocks, part = q_ref.shape[0] // BLOCK, part_refs[0].shape[0]
    seq_at, turn = here(part_rows)

    def part_of(p):
        return slice(p * part, (p + 1) * part)

    copies = start_copies(
        [*part_refs, q_any, do_any], [*(kv_ref.at[part_of(p)] for p in range(4)), q_ref, do_ref], sems
    )
    acc[...] = jnp.zeros_like(acc)
    dqt_ref[...] = jnp.zeros_like(dqt_ref)
    total[...] = total_in[...]
    delta[...] = delta_in[...]
    for copy in copies:
        copy.wait()

    def weigh(i, places, mask):
        keys = gathered(kv_ref, places, slice(0, HEAD))
        values = gathered(kv_ref, places, slice(HEAD, 2 * HEAD))
        rows = slice(0, len(places) * BLOCK)
        for h in range(0, GROUP, 2):
            lanes = slice(h * BLOCK, h * BLOCK + TILE)
            scores = by_rows(keys, heads(q_ref, i, h, 2))
            weights = jnp.exp2(scores * SCORE_SCALE - total[i, 0:1, lanes])
            if mask is not None:
                weights = jnp.where(mask, weights, 0.0)
            dweights = by_rows(values, heads(do_ref, i, h, 2))
            w_scr[rows, lanes] = weights.astype(BF16)
            ds_scr[rows, lanes] = (weights * (dweights - delta[i, 0:1, lanes])).astype(BF16)

    def spread(i, places):
        keys = gathered(kv_ref, places, slice(0, HEAD))
        rows = slice(0, len(places) * BLOCK)
        dk = plain(ds_scr[rows], heads(q_ref, i, 0, GROUP))
        dv = plain(w_scr[rows], heads(do_ref, i, 0, GROUP))
        dqt_ref[i] += plain(keys.T, ds_scr[rows])
        for n, p in enumerate(places):
            acc[rows_at(p), :HEAD] += dk[n * BLOCK : (n + 1) * BLOCK]
            acc[rows_at(p), HEAD:] += dv[n * BLOCK : (n + 1) * BLOCK]

    def one_block(i, carry):
        count = work[3 * local_blocks, 2 * local_blocks + i]

        def far_step(start, many, used):
            mask = allowed(many, used, turn, False)
            places = [work[local_blocks + i, start + e] for e in range(many)]
            first_pass(i, places, mask, q_ref, do_ref, kv_ref, total, delta)

        def places(start, many):
            return [work[2 * local_blocks + i, start + e] for e in range(many)]

        def begin(many):
            weigh(i, places(0, many), allowed(many, first, turn, True))
            spread(i, places(0, many))

        def body(n, carry):
            spread(i, places(first + 4 * n - 4, 4))
            weigh(i, places(first + 4 * n, 4), None)
            return carry

        sweep(work[3 * local_blocks, local_blocks + i], far_step)
        row_total = jnp.sum(total[i], 0, keepdims=True)
        row_delta = jnp.sum(delta[i], 0, keepdims=True) / row_total
        total[i] = jnp.broadcast_to(jnp.log2(row_total), (8, WIDE))
        delta[i] = jnp.broadcast_to(row_delta, (8, WIDE))
        first, quads = split(count)
        pl.when(first <= 2)(lambda: begin(2))
        pl.when(first > 2)(lambda: begin(4))

        @pl.when(quads > 0)
        def _():
            weigh(i, places(first, 4), None)
            lax.fori_loop(1, quads, body, 0)
            spread(i, places(first + 4 * quads - 4, 4))

        return carry

    lax.fori_loop(0, local_blocks, one_block, 0)
    for p in range(2):
        out_refs[p][...] = acc[part_of(p)].astype(BF16)
    span = q_ref.shape[0]
    middle = (seq_at >> 1) & (part // span - 1)
    for p in range(2, 4):
        for at in range(0, part, part_rows):
            m, row = at // span, at % span
            start = p * part + (m ^ middle) * span + (row ^ turn)
            rows = pl.ds(pl.multiple_of(start, part_rows), part_rows)
            out_refs[p][at : at + part_rows] = acc[rows].astype(BF16)


LIMIT = 32 << 20
SMEM = pl.BlockSpec(memory_space=pltpu.SMEM)
VMEM = pl.BlockSpec(memory_space=pltpu.VMEM)
ANY = pl.BlockSpec(memory_space=pl.ANY)


def resolve(lists, counts, spans, local_blocks, part):
    return pl.pallas_call(
        functools.partial(lists_kernel, part),
        in_specs=[SMEM] * 3,
        out_specs=SMEM,
        out_shape=jax.ShapeDtypeStruct((3 * local_blocks + 1, lists.shape[0] + 8), jnp.int32),
        scratch_shapes=[pltpu.SMEM(spans.shape, jnp.int32)],
        name="lists",
    )(lists, counts, spans)


def near_sums(part_rows, work, q, do, near, pair):
    local_blocks, rows = q.shape[0] // BLOCK, 2 * near.shape[0]
    return pl.pallas_call(
        functools.partial(near_kernel, part_rows),
        in_specs=[SMEM] + [ANY] * 4,
        out_specs=[VMEM] * 2,
        out_shape=[jax.ShapeDtypeStruct((local_blocks, 8, WIDE), F32)] * 2,
        scratch_shapes=[
            pltpu.VMEM(q.shape, BF16),
            pltpu.VMEM(do.shape, BF16),
            pltpu.VMEM((rows, 2 * HEAD), BF16),
            pltpu.SemaphoreType.DMA((4,)),
        ],
        compiler_params=pltpu.CompilerParams(vmem_limit_bytes=LIMIT),
        cost_estimate=pl.CostEstimate(flops=1 << 20, bytes_accessed=1 << 10, transcendentals=0),
        name="near",
    )(work, q, do, near, pair)


def attend(part_rows, work, q, do, total, delta, parts):
    local_blocks, rows = q.shape[0] // BLOCK, 4 * parts[0].shape[0]
    return pl.pallas_call(
        functools.partial(main_kernel, part_rows),
        in_specs=[SMEM] + [ANY] * 2 + [VMEM] * 2 + [ANY] * 4,
        out_specs=[VMEM] * 5,
        out_shape=[jax.ShapeDtypeStruct((local_blocks, HEAD, WIDE), F32)]
        + [jax.ShapeDtypeStruct(x.shape, BF16) for x in parts],
        scratch_shapes=[
            pltpu.VMEM(q.shape, BF16),
            pltpu.VMEM(do.shape, BF16),
            pltpu.VMEM((rows, 2 * HEAD), BF16),
            pltpu.VMEM((local_blocks, 8, WIDE), F32),
            pltpu.VMEM((local_blocks, 8, WIDE), F32),
            pltpu.VMEM((4 * BLOCK, WIDE), BF16),
            pltpu.VMEM((4 * BLOCK, WIDE), BF16),
            pltpu.VMEM((rows, 2 * HEAD), F32),
            pltpu.SemaphoreType.DMA((6,)),
        ],
        compiler_params=pltpu.CompilerParams(vmem_limit_bytes=LIMIT),
        name="attend",
    )(work, q, do, total, delta, *parts)


def shards(
    queries,
    key_vector_rows,
    value_vector_rows,
    output_gradient,
    key_lists,
    block_counts,
    span_table,
):
    seq_devices, kv_devices = lax.axis_size("seq"), lax.axis_size("kvh")
    seq_at, kv_at = lax.axis_index("seq"), lax.axis_index("kvh")
    per_kvh = key_vector_rows.shape[0]
    half, middles = seq_devices // 2, seq_devices // 4
    span_rows = kv_devices * per_kvh
    near_groups = [
        [
            (top * half + middle * 2 + core) * kv_devices + head
            for middle in range(middles)
            for head in range(kv_devices)
        ]
        for top in range(2)
        for core in range(2)
    ]

    def swap(x, seq_step, kv_step):
        if seq_step == 0 and kv_step == 0:
            return x
        pairs = [
            (s * kv_devices + h, (s ^ seq_step) * kv_devices + (h ^ kv_step))
            for s in range(seq_devices)
            for h in range(kv_devices)
        ]
        return lax.ppermute(x, ("seq", "kvh"), pairs)

    def exchange_near(x):
        x = x.reshape(middles * kv_devices, per_kvh, 2 * HEAD)
        return lax.all_to_all(x, ("seq", "kvh"), 0, 0, axis_index_groups=near_groups)

    work = resolve(key_lists.T, block_counts, span_table, queries.shape[0] // BLOCK, per_kvh)
    own = jnp.stack(
        [
            jnp.concatenate([x[:, h * HEAD : (h + 1) * HEAD] for x in (key_vector_rows, value_vector_rows)], 1)
            for h in range(kv_devices)
        ]
    )
    far = swap(own, half, 0)
    mine = [lax.dynamic_index_in_dim(own, kv_at ^ j, 0, False) for j in range(kv_devices)]
    near_span = jnp.concatenate([swap(mine[j], 0, j) for j in range(kv_devices)], 0)
    near_part = jnp.concatenate([swap(near_span, 2 * m, 0) for m in range(middles)], 0)
    near_pair = swap(near_part, 1, 0)
    far, work = lax.optimization_barrier((far, work))
    far_part = exchange_near(jnp.broadcast_to(far[None], (middles, *far.shape)))
    far_part = far_part.reshape(near_part.shape)

    common = (per_kvh, work, queries, output_gradient)
    total, delta = near_sums(*common, near_part, near_pair)
    total, far_part = lax.optimization_barrier((total, far_part))
    far_pair = swap(far_part, 1, 0)
    dqt, *partials = attend(*common, total, delta, [near_part, near_pair, far_part, far_pair])
    dq = jnp.transpose(dqt.reshape(-1, HEAD, GROUP, BLOCK), (0, 3, 2, 1)) * SCALE
    grad_queries = dq.reshape(queries.shape).astype(BF16)

    def chip_rows(kept, received, m):
        rows = slice(m * span_rows, (m + 1) * span_rows)
        return kept[rows].astype(F32) + received[rows].astype(F32)

    def sent_to_middles(kept, received):
        return [swap(chip_rows(kept, received, m).astype(BF16), 2 * m, 0) for m in range(1, middles)]

    def added(kept, received, others):
        return sum([x.astype(F32) for x in others], chip_rows(kept, received, 0))

    def to_owners(span, seq_step):
        pieces = [span[j * per_kvh : (j + 1) * per_kvh] for j in range(kv_devices)]
        return [
            x if seq_step + j == 0 else swap(x.astype(BF16), seq_step, j).astype(F32)
            for j, x in enumerate(pieces)
        ]

    far_received, near_received = swap(partials[3], 1, 0), swap(partials[1], 1, 0)
    far_others = sent_to_middles(partials[2], far_received)
    near_others = sent_to_middles(partials[0], near_received)
    far_sums = to_owners(added(partials[2], far_received, far_others), half)
    near_grads = to_owners(added(partials[0], near_received, near_others), 0)
    sums = jnp.stack([x + y for x, y in zip(near_grads, far_sums)])
    sums = [lax.dynamic_index_in_dim(sums, kv_at ^ h, 0, False) for h in range(kv_devices)]
    key_gradient = jnp.concatenate([x[:, :HEAD] * SCALE for x in sums], 1).astype(BF16)
    value_gradient = jnp.concatenate([x[:, HEAD:] for x in sums], 1).astype(BF16)
    return grad_queries, key_gradient, value_gradient


def solution(mesh):
    placed = (
        P("seq", "kvh"),
        P(("seq", "kvh"), None),
        P(("seq", "kvh"), None),
        P("seq", "kvh"),
        P(),
        P(),
        P(),
    )
    return jax.shard_map(
        shards,
        mesh=mesh,
        in_specs=placed,
        out_specs=(P("seq", "kvh"), P(("seq", "kvh"), None), P(("seq", "kvh"), None)),
        check_vma=False,
    )
```

```python
import functools

import jax
import jax.numpy as jnp
from jax import lax
from jax.experimental import pallas as pl
from jax.experimental.pallas import tpu as pltpu
from jax.sharding import PartitionSpec as P

HEAD = 128
GROUP = 8
BLOCK = 128
SCALE = HEAD ** (-0.5)
LOG2E = 1.4426950408889634
SCORE_SCALE = SCALE * LOG2E
TILE = 2 * BLOCK
WIDE = GROUP * BLOCK
BF16 = jnp.bfloat16
F32 = jnp.float32
BY_ROWS = (((1,), (1,)), ((), ()))


def by_rows(a, b):
    return lax.dot_general(a, b, BY_ROWS, preferred_element_type=F32)


def plain(a, b):
    return jnp.dot(a, b, preferred_element_type=F32)


def start_copies(sources, targets, sems):
    copies = [pltpu.make_async_copy(a, b, sems.at[n]) for n, (a, b) in enumerate(zip(sources, targets))]
    for copy in copies:
        copy.start()
    return copies


def here(part):
    return lax.axis_index("seq"), lax.axis_index("kvh") * part


def lists_kernel(part, lists, counts, spans, work, place):
    n_slots, local_blocks = spans.shape[0], (work.shape[0] - 1) // 3
    seq_at, turn = here(part)
    seq_bits = (n_slots // local_blocks).bit_length() - 1
    block_bits, half_bit = local_blocks.bit_length() - 1, seq_bits - 1
    part_bits = half_bit - 1 + block_bits

    def find(slot, carry):
        owner, block = slot >> block_bits, slot & (local_blocks - 1)
        apart = owner ^ seq_at
        is_far = apart >> half_bit
        middle = (jnp.where(is_far == 1, owner, apart) >> 1) & ((1 << (half_bit - 1)) - 1)
        block = jnp.where(is_far == 1, block, block ^ (turn >> 7))
        place[spans[slot]] = (((is_far << 1) | (apart & 1)) << part_bits) | (middle << block_bits) | block
        return carry

    lax.fori_loop(0, n_slots, find, 0, unroll=8)
    for i in range(local_blocks):
        at = spans[seq_at * local_blocks + i]
        near, far, every = (kind * local_blocks + i for kind in range(3))

        def clear(e, carry):
            for row in (near, far, every):
                work[row, e] = 0
            return carry

        def keep(e, sizes):
            found = place[lists[e, at]]
            is_far = found >> (part_bits + 1)
            work[near, sizes[0]] = found
            work[far, sizes[1]] = found
            work[every, e] = found
            return sizes[0] + 1 - is_far, sizes[1] + is_far

        lax.fori_loop(0, work.shape[1], clear, 0, unroll=8)
        near_size, far_size = lax.fori_loop(0, counts[at], keep, (0, 0))
        work[near, near_size] = 0
        work[far, far_size] = 0
        for kind, size in enumerate((near_size, far_size, counts[at])):
            work[3 * local_blocks, kind * local_blocks + i] = size


def heads(ref, i, first, many):
    rows = pl.ds(pl.multiple_of(i * BLOCK, BLOCK), BLOCK)
    return jnp.concatenate([ref[rows, h * HEAD : (h + 1) * HEAD] for h in range(first, first + many)], 0)


def rows_at(place):
    return pl.ds(pl.multiple_of(place * BLOCK, BLOCK), BLOCK)


def gathered(kv_ref, places, lanes):
    return jnp.concatenate([kv_ref[rows_at(p), lanes] for p in places], 0)


def allowed(many, count, turn, diagonal):
    if count is None:
        return None
    key_at = lax.broadcasted_iota(jnp.int32, (many * BLOCK, TILE), 0)
    entry = key_at // BLOCK
    mask = entry < count
    if diagonal:
        query_at = lax.broadcasted_iota(jnp.int32, (many * BLOCK, TILE), 1) & (BLOCK - 1)
        here = (key_at & (BLOCK - 1)) ^ (turn & (BLOCK - 1))
        mask = jnp.logical_and(mask, jnp.logical_or(entry > 0, here <= query_at))
    return mask


def split(count):
    first = (count + 3) % 4 + 1
    return first, (count - first) // 4


def sweep(count, step):
    first, quads = split(count)

    @pl.when(jnp.logical_and(count > 0, first <= 2))
    def _():
        step(0, 2, first)

    @pl.when(jnp.logical_and(count > 0, first > 2))
    def _():
        step(0, 4, first)

    def body(n, carry):
        step(first + 8 * n, 8, None)
        return carry

    lax.fori_loop(0, quads // 2, body, 0)

    @pl.when(jnp.logical_and(count > 0, quads % 2 == 1))
    def _():
        step(first + 4 * (quads - 1), 4, None)


def first_pass(i, places, mask, q_ref, do_ref, kv_ref, total, delta):
    keys = gathered(kv_ref, places, slice(0, HEAD))
    values = gathered(kv_ref, places, slice(HEAD, 2 * HEAD))
    for h in range(0, GROUP, 2):
        lanes = slice(h * BLOCK, h * BLOCK + TILE)
        expd = jnp.exp2(by_rows(keys, heads(q_ref, i, h, 2)) * SCORE_SCALE)
        if mask is not None:
            expd = jnp.where(mask, expd, 0.0)
        total[i, :, lanes] += jnp.sum(expd.reshape(-1, 8, TILE), 0)
        dweights = by_rows(values, heads(do_ref, i, h, 2))
        delta[i, :, lanes] += jnp.sum((expd * dweights).reshape(-1, 8, TILE), 0)


def near_kernel(part_rows, work, q_any, do_any, near_any, pair_any, total, delta, *scratch):
    q_ref, do_ref, kv_ref, sems = scratch
    local_blocks, part = q_ref.shape[0] // BLOCK, near_any.shape[0]
    _, turn = here(part_rows)
    copies = start_copies(
        [near_any, pair_any, q_any, do_any],
        [kv_ref.at[:part], kv_ref.at[part:], q_ref, do_ref],
        sems,
    )
    total[...] = jnp.zeros_like(total)
    delta[...] = jnp.zeros_like(delta)
    for copy in copies:
        copy.wait()

    def one_block(i, carry):
        def step(start, many, used):
            mask = allowed(many, used, turn, True)
            places = [work[i, start + e] for e in range(many)]
            first_pass(i, places, mask, q_ref, do_ref, kv_ref, total, delta)

        sweep(work[3 * local_blocks, i], step)
        return carry

    lax.fori_loop(0, local_blocks, one_block, 0)


def main_kernel(part_rows, work, q_any, do_any, total_in, delta_in, *refs):
    part_refs, (dqt_ref, *out_refs), scratch = refs[:4], refs[4:9], refs[9:]
    q_ref, do_ref, kv_ref, total, delta, w_scr, ds_scr, acc, sems = scratch
    local_blocks, part = q_ref.shape[0] // BLOCK, part_refs[0].shape[0]
    seq_at, turn = here(part_rows)

    def part_of(p):
        return slice(p * part, (p + 1) * part)

    copies = start_copies(
        [*part_refs, q_any, do_any], [*(kv_ref.at[part_of(p)] for p in range(4)), q_ref, do_ref], sems
    )
    acc[...] = jnp.zeros_like(acc)
    dqt_ref[...] = jnp.zeros_like(dqt_ref)
    total[...] = total_in[...]
    delta[...] = delta_in[...]
    for copy in copies:
        copy.wait()

    def weigh(i, places, mask):
        keys = gathered(kv_ref, places, slice(0, HEAD))
        values = gathered(kv_ref, places, slice(HEAD, 2 * HEAD))
        rows = slice(0, len(places) * BLOCK)
        for h in range(0, GROUP, 2):
            lanes = slice(h * BLOCK, h * BLOCK + TILE)
            scores = by_rows(keys, heads(q_ref, i, h, 2))
            weights = jnp.exp2(scores * SCORE_SCALE - total[i, 0:1, lanes])
            if mask is not None:
                weights = jnp.where(mask, weights, 0.0)
            dweights = by_rows(values, heads(do_ref, i, h, 2))
            w_scr[rows, lanes] = weights.astype(BF16)
            ds_scr[rows, lanes] = (weights * (dweights - delta[i, 0:1, lanes])).astype(BF16)

    def spread(i, places):
        keys = gathered(kv_ref, places, slice(0, HEAD))
        rows = slice(0, len(places) * BLOCK)
        dk = plain(ds_scr[rows], heads(q_ref, i, 0, GROUP))
        dv = plain(w_scr[rows], heads(do_ref, i, 0, GROUP))
        dqt_ref[i] += plain(keys.T, ds_scr[rows])
        for n, p in enumerate(places):
            acc[rows_at(p), :HEAD] += dk[n * BLOCK : (n + 1) * BLOCK]
            acc[rows_at(p), HEAD:] += dv[n * BLOCK : (n + 1) * BLOCK]

    def one_block(i, carry):
        count = work[3 * local_blocks, 2 * local_blocks + i]

        def far_step(start, many, used):
            mask = allowed(many, used, turn, False)
            places = [work[local_blocks + i, start + e] for e in range(many)]
            first_pass(i, places, mask, q_ref, do_ref, kv_ref, total, delta)

        def places(start, many):
            return [work[2 * local_blocks + i, start + e] for e in range(many)]

        def begin(many):
            weigh(i, places(0, many), allowed(many, first, turn, True))
            spread(i, places(0, many))

        sweep(work[3 * local_blocks, local_blocks + i], far_step)
        row_total = jnp.sum(total[i], 0, keepdims=True)
        row_delta = jnp.sum(delta[i], 0, keepdims=True) / row_total
        total[i] = jnp.broadcast_to(jnp.log2(row_total), (8, WIDE))
        delta[i] = jnp.broadcast_to(row_delta, (8, WIDE))
        first, quads = split(count)
        pl.when(first <= 2)(lambda: begin(2))
        pl.when(first > 2)(lambda: begin(4))
        start = first + 4 * (quads % 2)

        @pl.when(quads % 2 == 1)
        def _():
            weigh(i, places(first, 4), None)
            spread(i, places(first, 4))

        @pl.when(quads // 2 % 2 == 1)
        def _():
            weigh(i, places(start, 8), None)
            spread(i, places(start, 8))

        second = start + 8 * (quads // 2 % 2)

        def body(n, carry):
            weigh(i, places(second + 16 * n, 16), None)
            spread(i, places(second + 16 * n, 16))
            return carry

        lax.fori_loop(0, quads // 4, body, 0)

        return carry

    lax.fori_loop(0, local_blocks, one_block, 0)
    for p in range(2):
        out_refs[p][...] = acc[part_of(p)].astype(BF16)
    span = q_ref.shape[0]
    middle = (seq_at >> 1) & (part // span - 1)
    for p in range(2, 4):
        for at in range(0, part, part_rows):
            m, row = at // span, at % span
            start = p * part + (m ^ middle) * span + (row ^ turn)
            rows = pl.ds(pl.multiple_of(start, part_rows), part_rows)
            out_refs[p][at : at + part_rows] = acc[rows].astype(BF16)


LIMIT = 32 << 20
SMEM = pl.BlockSpec(memory_space=pltpu.SMEM)
VMEM = pl.BlockSpec(memory_space=pltpu.VMEM)
ANY = pl.BlockSpec(memory_space=pl.ANY)


def resolve(lists, counts, spans, local_blocks, part):
    return pl.pallas_call(
        functools.partial(lists_kernel, part),
        in_specs=[SMEM] * 3,
        out_specs=SMEM,
        out_shape=jax.ShapeDtypeStruct((3 * local_blocks + 1, lists.shape[0] + 8), jnp.int32),
        scratch_shapes=[pltpu.SMEM(spans.shape, jnp.int32)],
        name="lists",
    )(lists, counts, spans)


def near_sums(part_rows, work, q, do, near, pair):
    local_blocks, rows = q.shape[0] // BLOCK, 2 * near.shape[0]
    return pl.pallas_call(
        functools.partial(near_kernel, part_rows),
        in_specs=[SMEM] + [ANY] * 4,
        out_specs=[VMEM] * 2,
        out_shape=[jax.ShapeDtypeStruct((local_blocks, 8, WIDE), F32)] * 2,
        scratch_shapes=[
            pltpu.VMEM(q.shape, BF16),
            pltpu.VMEM(do.shape, BF16),
            pltpu.VMEM((rows, 2 * HEAD), BF16),
            pltpu.SemaphoreType.DMA((4,)),
        ],
        compiler_params=pltpu.CompilerParams(vmem_limit_bytes=LIMIT),
        cost_estimate=pl.CostEstimate(flops=1 << 20, bytes_accessed=1 << 10, transcendentals=0),
        name="near",
    )(work, q, do, near, pair)


def attend(part_rows, work, q, do, total, delta, parts):
    local_blocks, rows = q.shape[0] // BLOCK, 4 * parts[0].shape[0]
    return pl.pallas_call(
        functools.partial(main_kernel, part_rows),
        in_specs=[SMEM] + [ANY] * 2 + [VMEM] * 2 + [ANY] * 4,
        out_specs=[VMEM] * 5,
        out_shape=[jax.ShapeDtypeStruct((local_blocks, HEAD, WIDE), F32)]
        + [jax.ShapeDtypeStruct(x.shape, BF16) for x in parts],
        scratch_shapes=[
            pltpu.VMEM(q.shape, BF16),
            pltpu.VMEM(do.shape, BF16),
            pltpu.VMEM((rows, 2 * HEAD), BF16),
            pltpu.VMEM((local_blocks, 8, WIDE), F32),
            pltpu.VMEM((local_blocks, 8, WIDE), F32),
            pltpu.VMEM((16 * BLOCK, WIDE), BF16),
            pltpu.VMEM((16 * BLOCK, WIDE), BF16),
            pltpu.VMEM((rows, 2 * HEAD), F32),
            pltpu.SemaphoreType.DMA((6,)),
        ],
        compiler_params=pltpu.CompilerParams(vmem_limit_bytes=LIMIT),
        name="attend",
    )(work, q, do, total, delta, *parts)


def shards(
    queries,
    key_vector_rows,
    value_vector_rows,
    output_gradient,
    key_lists,
    block_counts,
    span_table,
):
    seq_devices, kv_devices = lax.axis_size("seq"), lax.axis_size("kvh")
    seq_at, kv_at = lax.axis_index("seq"), lax.axis_index("kvh")
    per_kvh = key_vector_rows.shape[0]
    half, middles = seq_devices // 2, seq_devices // 4
    span_rows = kv_devices * per_kvh
    near_groups = [
        [
            (top * half + middle * 2 + core) * kv_devices + head
            for middle in range(middles)
            for head in range(kv_devices)
        ]
        for top in range(2)
        for core in range(2)
    ]

    def swap(x, seq_step, kv_step):
        if seq_step == 0 and kv_step == 0:
            return x
        pairs = [
            (s * kv_devices + h, (s ^ seq_step) * kv_devices + (h ^ kv_step))
            for s in range(seq_devices)
            for h in range(kv_devices)
        ]
        return lax.ppermute(x, ("seq", "kvh"), pairs)

    def exchange_near(x):
        x = x.reshape(middles * kv_devices, per_kvh, 2 * HEAD)
        return lax.all_to_all(x, ("seq", "kvh"), 0, 0, axis_index_groups=near_groups)

    work = resolve(key_lists.T, block_counts, span_table, queries.shape[0] // BLOCK, per_kvh)
    own = jnp.stack(
        [
            jnp.concatenate([x[:, h * HEAD : (h + 1) * HEAD] for x in (key_vector_rows, value_vector_rows)], 1)
            for h in range(kv_devices)
        ]
    )
    far = swap(own, half, 0)
    mine = [lax.dynamic_index_in_dim(own, kv_at ^ j, 0, False) for j in range(kv_devices)]
    near_span = jnp.concatenate([swap(mine[j], 0, j) for j in range(kv_devices)], 0)
    near_part = jnp.concatenate([swap(near_span, 2 * m, 0) for m in range(middles)], 0)
    near_pair = swap(near_part, 1, 0)
    far, work = lax.optimization_barrier((far, work))
    far_part = exchange_near(jnp.broadcast_to(far[None], (middles, *far.shape)))
    far_part = far_part.reshape(near_part.shape)

    common = (per_kvh, work, queries, output_gradient)
    total, delta = near_sums(*common, near_part, near_pair)
    total, far_part = lax.optimization_barrier((total, far_part))
    far_pair = swap(far_part, 1, 0)
    dqt, *partials = attend(*common, total, delta, [near_part, near_pair, far_part, far_pair])
    dq = jnp.transpose(dqt.reshape(-1, HEAD, GROUP, BLOCK), (0, 3, 2, 1)) * SCALE
    grad_queries = dq.reshape(queries.shape).astype(BF16)

    def chip_rows(kept, received, m):
        rows = slice(m * span_rows, (m + 1) * span_rows)
        return kept[rows].astype(F32) + received[rows].astype(F32)

    def sent_to_middles(kept, received):
        return [swap(chip_rows(kept, received, m).astype(BF16), 2 * m, 0) for m in range(1, middles)]

    def added(kept, received, others):
        return sum([x.astype(F32) for x in others], chip_rows(kept, received, 0))

    def to_owners(span, seq_step):
        pieces = [span[j * per_kvh : (j + 1) * per_kvh] for j in range(kv_devices)]
        return [
            x if seq_step + j == 0 else swap(x.astype(BF16), seq_step, j).astype(F32)
            for j, x in enumerate(pieces)
        ]

    far_received, near_received = swap(partials[3], 1, 0), swap(partials[1], 1, 0)
    far_others = sent_to_middles(partials[2], far_received)
    near_others = sent_to_middles(partials[0], near_received)
    far_sums = to_owners(added(partials[2], far_received, far_others), half)
    near_grads = to_owners(added(partials[0], near_received, near_others), 0)
    sums = jnp.stack([x + y for x, y in zip(near_grads, far_sums)])
    sums = [lax.dynamic_index_in_dim(sums, kv_at ^ h, 0, False) for h in range(kv_devices)]
    key_gradient = jnp.concatenate([x[:, :HEAD] * SCALE for x in sums], 1).astype(BF16)
    value_gradient = jnp.concatenate([x[:, HEAD:] for x in sums], 1).astype(BF16)
    return grad_queries, key_gradient, value_gradient


def solution(mesh):
    placed = (
        P("seq", "kvh"),
        P(("seq", "kvh"), None),
        P(("seq", "kvh"), None),
        P("seq", "kvh"),
        P(),
        P(),
        P(),
    )
    return jax.shard_map(
        shards,
        mesh=mesh,
        in_specs=placed,
        out_specs=(P("seq", "kvh"), P(("seq", "kvh"), None), P(("seq", "kvh"), None)),
        check_vma=False,
    )
```

```python
import functools

import jax
import jax.numpy as jnp
from jax import lax
from jax.experimental import pallas as pl
from jax.experimental.pallas import tpu as pltpu
from jax.sharding import PartitionSpec as P

HEAD = 128
GROUP = 8
BLOCK = 128
SCALE = HEAD ** (-0.5)
LOG2E = 1.4426950408889634
SCORE_SCALE = SCALE * LOG2E
TILE = 2 * BLOCK
WIDE = GROUP * BLOCK
BF16 = jnp.bfloat16
F32 = jnp.float32
BY_ROWS = (((1,), (1,)), ((), ()))


def by_rows(a, b):
    return lax.dot_general(a, b, BY_ROWS, preferred_element_type=F32)


def plain(a, b):
    return jnp.dot(a, b, preferred_element_type=F32)


def start_copies(sources, targets, sems):
    copies = [pltpu.make_async_copy(a, b, sems.at[n]) for n, (a, b) in enumerate(zip(sources, targets))]
    for copy in copies:
        copy.start()
    return copies


def here(part):
    return lax.axis_index("seq"), lax.axis_index("kvh") * part


def lists_kernel(part, lists, counts, spans, work, place):
    n_slots, local_blocks = spans.shape[0], (work.shape[0] - 1) // 3
    seq_at, turn = here(part)
    seq_bits = (n_slots // local_blocks).bit_length() - 1
    block_bits, half_bit = local_blocks.bit_length() - 1, seq_bits - 1
    part_bits = half_bit - 1 + block_bits

    def find(slot, carry):
        owner, block = slot >> block_bits, slot & (local_blocks - 1)
        apart = owner ^ seq_at
        is_far = apart >> half_bit
        middle = (jnp.where(is_far == 1, owner, apart) >> 1) & ((1 << (half_bit - 1)) - 1)
        block = jnp.where(is_far == 1, block, block ^ (turn >> 7))
        place[spans[slot]] = (((is_far << 1) | (apart & 1)) << part_bits) | (middle << block_bits) | block
        return carry

    lax.fori_loop(0, n_slots, find, 0, unroll=8)
    for i in range(local_blocks):
        at = spans[seq_at * local_blocks + i]
        near, far, every = (kind * local_blocks + i for kind in range(3))

        def clear(e, carry):
            for row in (near, far, every):
                work[row, e] = 0
            return carry

        def keep(e, sizes):
            found = place[lists[e, at]]
            is_far = found >> (part_bits + 1)
            work[near, sizes[0]] = found
            work[far, sizes[1]] = found
            work[every, e] = found
            return sizes[0] + 1 - is_far, sizes[1] + is_far

        lax.fori_loop(0, work.shape[1], clear, 0, unroll=8)
        near_size, far_size = lax.fori_loop(0, counts[at], keep, (0, 0))
        work[near, near_size] = 0
        work[far, far_size] = 0
        for kind, size in enumerate((near_size, far_size, counts[at])):
            work[3 * local_blocks, kind * local_blocks + i] = size


def heads(ref, i, first, many):
    rows = pl.ds(pl.multiple_of(i * BLOCK, BLOCK), BLOCK)
    return jnp.concatenate([ref[rows, h * HEAD : (h + 1) * HEAD] for h in range(first, first + many)], 0)


def rows_at(place):
    return pl.ds(pl.multiple_of(place * BLOCK, BLOCK), BLOCK)


def gathered(kv_ref, places, lanes):
    return jnp.concatenate([kv_ref[rows_at(p), lanes] for p in places], 0)


def allowed(many, count, turn, diagonal):
    if count is None:
        return None
    key_at = lax.broadcasted_iota(jnp.int32, (many * BLOCK, TILE), 0)
    entry = key_at // BLOCK
    mask = entry < count
    if diagonal:
        query_at = lax.broadcasted_iota(jnp.int32, (many * BLOCK, TILE), 1) & (BLOCK - 1)
        here = (key_at & (BLOCK - 1)) ^ (turn & (BLOCK - 1))
        mask = jnp.logical_and(mask, jnp.logical_or(entry > 0, here <= query_at))
    return mask


def split(count):
    first = (count + 3) % 4 + 1
    return first, (count - first) // 4


def sweep(count, step):
    first, quads = split(count)

    @pl.when(jnp.logical_and(count > 0, first <= 2))
    def _():
        step(0, 2, first)

    @pl.when(jnp.logical_and(count > 0, first > 2))
    def _():
        step(0, 4, first)

    def body(n, carry):
        step(first + 8 * n, 8, None)
        return carry

    lax.fori_loop(0, quads // 2, body, 0)

    @pl.when(jnp.logical_and(count > 0, quads % 2 == 1))
    def _():
        step(first + 4 * (quads - 1), 4, None)


def first_pass(i, places, mask, q_ref, do_ref, kv_ref, total, delta):
    keys = gathered(kv_ref, places, slice(0, HEAD))
    values = gathered(kv_ref, places, slice(HEAD, 2 * HEAD))
    for h in range(0, GROUP, 2):
        lanes = slice(h * BLOCK, h * BLOCK + TILE)
        expd = jnp.exp2(by_rows(keys, heads(q_ref, i, h, 2)) * SCORE_SCALE)
        if mask is not None:
            expd = jnp.where(mask, expd, 0.0)
        total[i, :, lanes] += jnp.sum(expd.reshape(-1, 8, TILE), 0)
        dweights = by_rows(values, heads(do_ref, i, h, 2))
        delta[i, :, lanes] += jnp.sum((expd * dweights).reshape(-1, 8, TILE), 0)


def near_kernel(part_rows, work, q_any, do_any, near_any, pair_any, total, delta, *scratch):
    q_ref, do_ref, kv_ref, sems = scratch
    local_blocks, part = q_ref.shape[0] // BLOCK, near_any.shape[0]
    _, turn = here(part_rows)
    copies = start_copies(
        [near_any, pair_any, q_any, do_any],
        [kv_ref.at[:part], kv_ref.at[part:], q_ref, do_ref],
        sems,
    )
    total[...] = jnp.zeros_like(total)
    delta[...] = jnp.zeros_like(delta)
    for copy in copies:
        copy.wait()

    def one_block(i, carry):
        def step(start, many, used):
            mask = allowed(many, used, turn, True)
            places = [work[i, start + e] for e in range(many)]
            first_pass(i, places, mask, q_ref, do_ref, kv_ref, total, delta)

        sweep(work[3 * local_blocks, i], step)
        return carry

    lax.fori_loop(0, local_blocks, one_block, 0)


def main_kernel(part_rows, work, q_any, do_any, total_in, delta_in, *refs):
    part_refs, (dqt_ref, *out_refs), scratch = refs[:4], refs[4:9], refs[9:]
    q_ref, do_ref, kv_ref, total, delta, w_scr, ds_scr, acc, sems = scratch
    local_blocks, part = q_ref.shape[0] // BLOCK, part_refs[0].shape[0]
    seq_at, turn = here(part_rows)

    def part_of(p):
        return slice(p * part, (p + 1) * part)

    copies = start_copies(
        [*part_refs, q_any, do_any], [*(kv_ref.at[part_of(p)] for p in range(4)), q_ref, do_ref], sems
    )
    acc[...] = jnp.zeros_like(acc)
    dqt_ref[...] = jnp.zeros_like(dqt_ref)
    total[...] = total_in[...]
    delta[...] = delta_in[...]
    for copy in copies:
        copy.wait()

    def weigh(i, places, mask):
        keys = gathered(kv_ref, places, slice(0, HEAD))
        values = gathered(kv_ref, places, slice(HEAD, 2 * HEAD))
        rows = slice(0, len(places) * BLOCK)
        for h in range(0, GROUP, 2):
            lanes = slice(h * BLOCK, h * BLOCK + TILE)
            scores = by_rows(keys, heads(q_ref, i, h, 2))
            weights = jnp.exp2(scores * SCORE_SCALE - total[i, 0:1, lanes])
            if mask is not None:
                weights = jnp.where(mask, weights, 0.0)
            dweights = by_rows(values, heads(do_ref, i, h, 2))
            w_scr[rows, lanes] = weights.astype(BF16)
            ds_scr[rows, lanes] = (weights * (dweights - delta[i, 0:1, lanes])).astype(BF16)

    def spread(i, places):
        keys = gathered(kv_ref, places, slice(0, HEAD))
        rows = slice(0, len(places) * BLOCK)
        dk = plain(ds_scr[rows], heads(q_ref, i, 0, GROUP))
        dv = plain(w_scr[rows], heads(do_ref, i, 0, GROUP))
        dqt_ref[i] += plain(keys.T, ds_scr[rows])
        for n, p in enumerate(places):
            acc[rows_at(p), :HEAD] += dk[n * BLOCK : (n + 1) * BLOCK]
            acc[rows_at(p), HEAD:] += dv[n * BLOCK : (n + 1) * BLOCK]

    def one_block(i, carry):
        count = work[3 * local_blocks, 2 * local_blocks + i]

        def far_step(start, many, used):
            mask = allowed(many, used, turn, False)
            places = [work[local_blocks + i, start + e] for e in range(many)]
            first_pass(i, places, mask, q_ref, do_ref, kv_ref, total, delta)

        def places(start, many):
            return [work[2 * local_blocks + i, start + e] for e in range(many)]

        def begin(many):
            weigh(i, places(0, many), allowed(many, first, turn, True))
            spread(i, places(0, many))

        sweep(work[3 * local_blocks, local_blocks + i], far_step)
        row_total = jnp.sum(total[i], 0, keepdims=True)
        row_delta = jnp.sum(delta[i], 0, keepdims=True) / row_total
        total[i] = jnp.broadcast_to(jnp.log2(row_total), (8, WIDE))
        delta[i] = jnp.broadcast_to(row_delta, (8, WIDE))
        first, quads = split(count)
        pl.when(first <= 2)(lambda: begin(2))
        pl.when(first > 2)(lambda: begin(4))
        start = first + 4 * (quads % 2)

        @pl.when(quads % 2 == 1)
        def _():
            weigh(i, places(first, 4), None)
            spread(i, places(first, 4))

        @pl.when(quads // 2 % 2 == 1)
        def _():
            weigh(i, places(start, 8), None)
            spread(i, places(start, 8))

        second = start + 8 * (quads // 2 % 2)

        def body(n, carry):
            weigh(i, places(second + 16 * n, 16), None)
            spread(i, places(second + 16 * n, 16))
            return carry

        lax.fori_loop(0, quads // 4, body, 0)

        return carry

    lax.fori_loop(0, local_blocks, one_block, 0)
    for p in range(2):
        out_refs[p][...] = acc[part_of(p)].astype(BF16)
    span = q_ref.shape[0]
    middle = (seq_at >> 1) & (part // span - 1)
    for p in range(2, 4):
        for at in range(0, part, part_rows):
            m, row = at // span, at % span
            start = p * part + (m ^ middle) * span + (row ^ turn)
            rows = pl.ds(pl.multiple_of(start, part_rows), part_rows)
            out_refs[p][at : at + part_rows] = acc[rows].astype(BF16)


LIMIT = 32 << 20
SMEM = pl.BlockSpec(memory_space=pltpu.SMEM)
VMEM = pl.BlockSpec(memory_space=pltpu.VMEM)
ANY = pl.BlockSpec(memory_space=pl.ANY)


def resolve(lists, counts, spans, local_blocks, part):
    return pl.pallas_call(
        functools.partial(lists_kernel, part),
        in_specs=[SMEM] * 3,
        out_specs=SMEM,
        out_shape=jax.ShapeDtypeStruct((3 * local_blocks + 1, lists.shape[0] + 8), jnp.int32),
        scratch_shapes=[pltpu.SMEM(spans.shape, jnp.int32)],
        name="lists",
    )(lists, counts, spans)


def near_sums(part_rows, work, q, do, near, pair):
    local_blocks, rows = q.shape[0] // BLOCK, 2 * near.shape[0]
    return pl.pallas_call(
        functools.partial(near_kernel, part_rows),
        in_specs=[SMEM] + [ANY] * 4,
        out_specs=[VMEM] * 2,
        out_shape=[jax.ShapeDtypeStruct((local_blocks, 8, WIDE), F32)] * 2,
        scratch_shapes=[
            pltpu.VMEM(q.shape, BF16),
            pltpu.VMEM(do.shape, BF16),
            pltpu.VMEM((rows, 2 * HEAD), BF16),
            pltpu.SemaphoreType.DMA((4,)),
        ],
        compiler_params=pltpu.CompilerParams(vmem_limit_bytes=LIMIT),
        cost_estimate=pl.CostEstimate(flops=1 << 20, bytes_accessed=1 << 10, transcendentals=0),
        name="near",
    )(work, q, do, near, pair)


def attend(part_rows, work, q, do, total, delta, parts):
    local_blocks, rows = q.shape[0] // BLOCK, 4 * parts[0].shape[0]
    return pl.pallas_call(
        functools.partial(main_kernel, part_rows),
        in_specs=[SMEM] + [ANY] * 2 + [VMEM] * 2 + [ANY] * 4,
        out_specs=[VMEM] * 5,
        out_shape=[jax.ShapeDtypeStruct((local_blocks, HEAD, WIDE), F32)]
        + [jax.ShapeDtypeStruct(x.shape, BF16) for x in parts],
        scratch_shapes=[
            pltpu.VMEM(q.shape, BF16),
            pltpu.VMEM(do.shape, BF16),
            pltpu.VMEM((rows, 2 * HEAD), BF16),
            pltpu.VMEM((local_blocks, 8, WIDE), F32),
            pltpu.VMEM((local_blocks, 8, WIDE), F32),
            pltpu.VMEM((16 * BLOCK, WIDE), BF16),
            pltpu.VMEM((16 * BLOCK, WIDE), BF16),
            pltpu.VMEM((rows, 2 * HEAD), F32),
            pltpu.SemaphoreType.DMA((6,)),
        ],
        compiler_params=pltpu.CompilerParams(vmem_limit_bytes=LIMIT),
        name="attend",
    )(work, q, do, total, delta, *parts)


def shards(
    queries,
    key_vector_rows,
    value_vector_rows,
    output_gradient,
    key_lists,
    block_counts,
    span_table,
):
    seq_devices, kv_devices = lax.axis_size("seq"), lax.axis_size("kvh")
    seq_at, kv_at = lax.axis_index("seq"), lax.axis_index("kvh")
    per_kvh = key_vector_rows.shape[0]
    half, middles = seq_devices // 2, seq_devices // 4
    span_rows = kv_devices * per_kvh
    near_groups = [
        [
            (top * half + middle * 2 + core) * kv_devices + head
            for middle in range(middles)
            for head in range(kv_devices)
        ]
        for top in range(2)
        for core in range(2)
    ]

    def swap(x, seq_step, kv_step):
        if seq_step == 0 and kv_step == 0:
            return x
        pairs = [
            (s * kv_devices + h, (s ^ seq_step) * kv_devices + (h ^ kv_step))
            for s in range(seq_devices)
            for h in range(kv_devices)
        ]
        return lax.ppermute(x, ("seq", "kvh"), pairs)

    def exchange_near(x):
        x = x.reshape(middles * kv_devices, per_kvh, 2 * HEAD)
        return lax.all_to_all(x, ("seq", "kvh"), 0, 0, axis_index_groups=near_groups)

    work = resolve(key_lists.T, block_counts, span_table, queries.shape[0] // BLOCK, per_kvh)
    own = jnp.stack(
        [
            jnp.concatenate([x[:, h * HEAD : (h + 1) * HEAD] for x in (key_vector_rows, value_vector_rows)], 1)
            for h in range(kv_devices)
        ]
    )
    far = swap(own, half, 0)
    mine = [lax.dynamic_index_in_dim(own, kv_at ^ j, 0, False) for j in range(kv_devices)]
    near_span = jnp.concatenate([swap(mine[j], 0, j) for j in range(kv_devices)], 0)
    near_part = jnp.concatenate([swap(near_span, 2 * m, 0) for m in range(middles)], 0)
    near_pair = swap(near_part, 1, 0)
    far, work = lax.optimization_barrier((far, work))
    far_part = exchange_near(jnp.broadcast_to(far[None], (middles, *far.shape)))
    far_part = far_part.reshape(near_part.shape)

    common = (per_kvh, work, queries, output_gradient)
    total, delta = near_sums(*common, near_part, near_pair)
    total, far_part = lax.optimization_barrier((total, far_part))
    far_pair = swap(far_part, 1, 0)
    dqt, *partials = attend(*common, total, delta, [near_part, near_pair, far_part, far_pair])

    def chip_rows(kept, received, m):
        rows = slice(m * span_rows, (m + 1) * span_rows)
        return kept[rows].astype(F32) + received[rows].astype(F32)

    def sent_to_middles(kept, received):
        return [swap(chip_rows(kept, received, m).astype(BF16), 2 * m, 0) for m in range(1, middles)]

    def added(kept, received, others):
        return sum([x.astype(F32) for x in others], chip_rows(kept, received, 0))

    def to_owners(span, seq_step):
        pieces = [span[j * per_kvh : (j + 1) * per_kvh] for j in range(kv_devices)]
        return [
            x if seq_step + j == 0 else swap(x.astype(BF16), seq_step, j).astype(F32)
            for j, x in enumerate(pieces)
        ]

    far_received, near_received = swap(partials[3], 1, 0), swap(partials[1], 1, 0)
    far_others = sent_to_middles(partials[2], far_received)
    dqt, *far_others = lax.optimization_barrier((dqt, *far_others))
    dq = jnp.transpose(dqt.reshape(-1, HEAD, GROUP, BLOCK), (0, 3, 2, 1)) * SCALE
    grad_queries = dq.reshape(queries.shape).astype(BF16)
    near_others = sent_to_middles(partials[0], near_received)
    far_sums = to_owners(added(partials[2], far_received, far_others), half)
    near_grads = to_owners(added(partials[0], near_received, near_others), 0)
    sums = jnp.stack([x + y for x, y in zip(near_grads, far_sums)])
    sums = [lax.dynamic_index_in_dim(sums, kv_at ^ h, 0, False) for h in range(kv_devices)]
    key_gradient = jnp.concatenate([x[:, :HEAD] * SCALE for x in sums], 1).astype(BF16)
    value_gradient = jnp.concatenate([x[:, HEAD:] for x in sums], 1).astype(BF16)
    return grad_queries, key_gradient, value_gradient


def solution(mesh):
    placed = (
        P("seq", "kvh"),
        P(("seq", "kvh"), None),
        P(("seq", "kvh"), None),
        P("seq", "kvh"),
        P(),
        P(),
        P(),
    )
    return jax.shard_map(
        shards,
        mesh=mesh,
        in_specs=placed,
        out_specs=(P("seq", "kvh"), P(("seq", "kvh"), None), P(("seq", "kvh"), None)),
        check_vma=False,
    )
```

```python
import functools

import jax
import jax.numpy as jnp
from jax import lax
from jax.experimental import pallas as pl
from jax.experimental.pallas import tpu as pltpu
from jax.sharding import PartitionSpec as P

HEAD = 128
GROUP = 8
BLOCK = 128
SCALE = HEAD ** (-0.5)
LOG2E = 1.4426950408889634
SCORE_SCALE = SCALE * LOG2E
TILE = 2 * BLOCK
WIDE = GROUP * BLOCK
BF16 = jnp.bfloat16
F32 = jnp.float32
BY_ROWS = (((1,), (1,)), ((), ()))


def by_rows(a, b):
    return lax.dot_general(a, b, BY_ROWS, preferred_element_type=F32)


def plain(a, b):
    return jnp.dot(a, b, preferred_element_type=F32)


def start_copies(sources, targets, sems):
    copies = [pltpu.make_async_copy(a, b, sems.at[n]) for n, (a, b) in enumerate(zip(sources, targets))]
    for copy in copies:
        copy.start()
    return copies


def here(part):
    return lax.axis_index("seq"), lax.axis_index("kvh") * part


def lists_kernel(part, lists, counts, spans, work, place):
    n_slots, local_blocks = spans.shape[0], (work.shape[0] - 1) // 3
    seq_at, turn = here(part)
    seq_bits = (n_slots // local_blocks).bit_length() - 1
    block_bits, half_bit = local_blocks.bit_length() - 1, seq_bits - 1
    part_bits = half_bit - 1 + block_bits

    def find(slot, carry):
        owner, block = slot >> block_bits, slot & (local_blocks - 1)
        apart = owner ^ seq_at
        is_far = apart >> half_bit
        middle = (jnp.where(is_far == 1, owner, apart) >> 1) & ((1 << (half_bit - 1)) - 1)
        block = jnp.where(is_far == 1, block, block ^ (turn >> 7))
        place[spans[slot]] = (((is_far << 1) | (apart & 1)) << part_bits) | (middle << block_bits) | block
        return carry

    lax.fori_loop(0, n_slots, find, 0, unroll=8)
    for i in range(local_blocks):
        at = spans[seq_at * local_blocks + i]
        near, far, every = (kind * local_blocks + i for kind in range(3))

        def clear(e, carry):
            for row in (near, far, every):
                work[row, e] = 0
            return carry

        def keep(e, sizes):
            found = place[lists[e, at]]
            is_far = found >> (part_bits + 1)
            work[near, sizes[0]] = found
            work[far, sizes[1]] = found
            work[every, e] = found
            return sizes[0] + 1 - is_far, sizes[1] + is_far

        lax.fori_loop(0, work.shape[1], clear, 0, unroll=8)
        near_size, far_size = lax.fori_loop(0, counts[at], keep, (0, 0))
        work[near, near_size] = 0
        work[far, far_size] = 0
        for kind, size in enumerate((near_size, far_size, counts[at])):
            work[3 * local_blocks, kind * local_blocks + i] = size


def heads(ref, i, first, many):
    rows = pl.ds(pl.multiple_of(i * BLOCK, BLOCK), BLOCK)
    return jnp.concatenate([ref[rows, h * HEAD : (h + 1) * HEAD] for h in range(first, first + many)], 0)


def rows_at(place):
    return pl.ds(pl.multiple_of(place * BLOCK, BLOCK), BLOCK)


def gathered(kv_ref, places, lanes):
    return jnp.concatenate([kv_ref[rows_at(p), lanes] for p in places], 0)


def allowed(many, count, turn, diagonal):
    if count is None:
        return None
    key_at = lax.broadcasted_iota(jnp.int32, (many * BLOCK, TILE), 0)
    entry = key_at // BLOCK
    mask = entry < count
    if diagonal:
        query_at = lax.broadcasted_iota(jnp.int32, (many * BLOCK, TILE), 1) & (BLOCK - 1)
        here = (key_at & (BLOCK - 1)) ^ (turn & (BLOCK - 1))
        mask = jnp.logical_and(mask, jnp.logical_or(entry > 0, here <= query_at))
    return mask


def split(count):
    first = (count + 3) % 4 + 1
    return first, (count - first) // 4


def sweep(count, step):
    first, quads = split(count)

    @pl.when(jnp.logical_and(count > 0, first <= 2))
    def _():
        step(0, 2, first)

    @pl.when(jnp.logical_and(count > 0, first > 2))
    def _():
        step(0, 4, first)

    def body(n, carry):
        step(first + 8 * n, 8, None)
        return carry

    lax.fori_loop(0, quads // 2, body, 0)

    @pl.when(jnp.logical_and(count > 0, quads % 2 == 1))
    def _():
        step(first + 4 * (quads - 1), 4, None)


def first_pass(i, places, mask, q_ref, do_ref, kv_ref, total, delta):
    keys = gathered(kv_ref, places, slice(0, HEAD))
    values = gathered(kv_ref, places, slice(HEAD, 2 * HEAD))
    for h in range(0, GROUP, 2):
        lanes = slice(h * BLOCK, h * BLOCK + TILE)
        expd = jnp.exp2(by_rows(keys, heads(q_ref, i, h, 2)) * SCORE_SCALE)
        if mask is not None:
            expd = jnp.where(mask, expd, 0.0)
        total[i, :, lanes] += jnp.sum(expd.reshape(-1, 8, TILE), 0)
        dweights = by_rows(values, heads(do_ref, i, h, 2))
        delta[i, :, lanes] += jnp.sum((expd * dweights).reshape(-1, 8, TILE), 0)


def near_kernel(part_rows, work, q_any, do_any, near_any, pair_any, total, delta, *scratch):
    q_ref, do_ref, kv_ref, sems = scratch
    local_blocks, part = q_ref.shape[0] // BLOCK, near_any.shape[0]
    _, turn = here(part_rows)
    copies = start_copies(
        [near_any, pair_any, q_any, do_any],
        [kv_ref.at[:part], kv_ref.at[part:], q_ref, do_ref],
        sems,
    )
    total[...] = jnp.zeros_like(total)
    delta[...] = jnp.zeros_like(delta)
    for copy in copies:
        copy.wait()

    def one_block(i, carry):
        def step(start, many, used):
            mask = allowed(many, used, turn, True)
            places = [work[i, start + e] for e in range(many)]
            first_pass(i, places, mask, q_ref, do_ref, kv_ref, total, delta)

        sweep(work[3 * local_blocks, i], step)
        return carry

    lax.fori_loop(0, local_blocks, one_block, 0)


def main_kernel(part_rows, work, q_any, do_any, total_in, delta_in, *refs):
    part_refs, (dqt_ref, *out_refs), scratch = refs[:4], refs[4:9], refs[9:]
    q_ref, do_ref, kv_ref, total, delta, w_scr, ds_scr, acc, sems = scratch
    local_blocks, part = q_ref.shape[0] // BLOCK, part_refs[0].shape[0]
    seq_at, turn = here(part_rows)

    def part_of(p):
        return slice(p * part, (p + 1) * part)

    copies = start_copies(
        [*part_refs, q_any, do_any], [*(kv_ref.at[part_of(p)] for p in range(4)), q_ref, do_ref], sems
    )
    acc[...] = jnp.zeros_like(acc)
    dqt_ref[...] = jnp.zeros_like(dqt_ref)
    total[...] = total_in[...]
    delta[...] = delta_in[...]
    for copy in copies:
        copy.wait()

    def weigh(i, places, mask):
        keys = gathered(kv_ref, places, slice(0, HEAD))
        values = gathered(kv_ref, places, slice(HEAD, 2 * HEAD))
        rows = slice(0, len(places) * BLOCK)
        for h in range(0, GROUP, 2):
            lanes = slice(h * BLOCK, h * BLOCK + TILE)
            scores = by_rows(keys, heads(q_ref, i, h, 2))
            weights = jnp.exp2(scores * SCORE_SCALE - total[i, 0:1, lanes])
            if mask is not None:
                weights = jnp.where(mask, weights, 0.0)
            dweights = by_rows(values, heads(do_ref, i, h, 2))
            w_scr[rows, lanes] = weights.astype(BF16)
            ds_scr[rows, lanes] = (weights * (dweights - delta[i, 0:1, lanes])).astype(BF16)

    def spread(i, places):
        keys = gathered(kv_ref, places, slice(0, HEAD))
        rows = slice(0, len(places) * BLOCK)
        dk = plain(ds_scr[rows], heads(q_ref, i, 0, GROUP))
        dv = plain(w_scr[rows], heads(do_ref, i, 0, GROUP))
        dqt_ref[i] += plain(keys.T, ds_scr[rows])
        for n, p in enumerate(places):
            acc[rows_at(p), :HEAD] += dk[n * BLOCK : (n + 1) * BLOCK]
            acc[rows_at(p), HEAD:] += dv[n * BLOCK : (n + 1) * BLOCK]

    def one_block(i, carry):
        count = work[3 * local_blocks, 2 * local_blocks + i]

        def far_step(start, many, used):
            mask = allowed(many, used, turn, False)
            places = [work[local_blocks + i, start + e] for e in range(many)]
            first_pass(i, places, mask, q_ref, do_ref, kv_ref, total, delta)

        def places(start, many):
            return [work[2 * local_blocks + i, start + e] for e in range(many)]

        def begin(many):
            weigh(i, places(0, many), allowed(many, first, turn, True))
            spread(i, places(0, many))

        sweep(work[3 * local_blocks, local_blocks + i], far_step)
        row_total = jnp.sum(total[i], 0, keepdims=True)
        row_delta = jnp.sum(delta[i], 0, keepdims=True) / row_total
        total[i] = jnp.broadcast_to(jnp.log2(row_total), (8, WIDE))
        delta[i] = jnp.broadcast_to(row_delta, (8, WIDE))
        first, quads = split(count)
        pl.when(first <= 2)(lambda: begin(2))
        pl.when(first > 2)(lambda: begin(4))
        start = first + 4 * (quads % 2)

        @pl.when(quads % 2 == 1)
        def _():
            weigh(i, places(first, 4), None)
            spread(i, places(first, 4))

        @pl.when(quads // 2 % 2 == 1)
        def _():
            weigh(i, places(start, 8), None)
            spread(i, places(start, 8))

        second = start + 8 * (quads // 2 % 2)

        def body(n, carry):
            weigh(i, places(second + 16 * n, 16), None)
            spread(i, places(second + 16 * n, 16))
            return carry

        lax.fori_loop(0, quads // 4, body, 0)

        return carry

    lax.fori_loop(0, local_blocks, one_block, 0)
    for p in range(2):
        out_refs[p][...] = acc[part_of(p)].astype(BF16)
    span = q_ref.shape[0]
    middle = (seq_at >> 1) & (part // span - 1)
    for p in range(2, 4):
        for at in range(0, part, part_rows):
            m, row = at // span, at % span
            start = p * part + (m ^ middle) * span + (row ^ turn)
            rows = pl.ds(pl.multiple_of(start, part_rows), part_rows)
            out_refs[p][at : at + part_rows] = acc[rows].astype(BF16)


LIMIT = 32 << 20
SMEM = pl.BlockSpec(memory_space=pltpu.SMEM)
VMEM = pl.BlockSpec(memory_space=pltpu.VMEM)
ANY = pl.BlockSpec(memory_space=pl.ANY)


def resolve(lists, counts, spans, local_blocks, part):
    return pl.pallas_call(
        functools.partial(lists_kernel, part),
        in_specs=[SMEM] * 3,
        out_specs=SMEM,
        out_shape=jax.ShapeDtypeStruct((3 * local_blocks + 1, lists.shape[0] + 8), jnp.int32),
        scratch_shapes=[pltpu.SMEM(spans.shape, jnp.int32)],
        name="lists",
    )(lists, counts, spans)


def near_sums(part_rows, work, q, do, near, pair):
    local_blocks, rows = q.shape[0] // BLOCK, 2 * near.shape[0]
    return pl.pallas_call(
        functools.partial(near_kernel, part_rows),
        in_specs=[SMEM] + [ANY] * 4,
        out_specs=[VMEM] * 2,
        out_shape=[jax.ShapeDtypeStruct((local_blocks, 8, WIDE), F32)] * 2,
        scratch_shapes=[
            pltpu.VMEM(q.shape, BF16),
            pltpu.VMEM(do.shape, BF16),
            pltpu.VMEM((rows, 2 * HEAD), BF16),
            pltpu.SemaphoreType.DMA((4,)),
        ],
        compiler_params=pltpu.CompilerParams(vmem_limit_bytes=LIMIT),
        cost_estimate=pl.CostEstimate(flops=1 << 20, bytes_accessed=1 << 10, transcendentals=0),
        name="near",
    )(work, q, do, near, pair)


def attend(part_rows, work, q, do, total, delta, parts):
    local_blocks, rows = q.shape[0] // BLOCK, 4 * parts[0].shape[0]
    return pl.pallas_call(
        functools.partial(main_kernel, part_rows),
        in_specs=[SMEM] + [ANY] * 2 + [VMEM] * 2 + [ANY] * 4,
        out_specs=[VMEM] * 5,
        out_shape=[jax.ShapeDtypeStruct((local_blocks, HEAD, WIDE), F32)]
        + [jax.ShapeDtypeStruct(x.shape, BF16) for x in parts],
        scratch_shapes=[
            pltpu.VMEM(q.shape, BF16),
            pltpu.VMEM(do.shape, BF16),
            pltpu.VMEM((rows, 2 * HEAD), BF16),
            pltpu.VMEM((local_blocks, 8, WIDE), F32),
            pltpu.VMEM((local_blocks, 8, WIDE), F32),
            pltpu.VMEM((16 * BLOCK, WIDE), BF16),
            pltpu.VMEM((16 * BLOCK, WIDE), BF16),
            pltpu.VMEM((rows, 2 * HEAD), F32),
            pltpu.SemaphoreType.DMA((6,)),
        ],
        compiler_params=pltpu.CompilerParams(vmem_limit_bytes=LIMIT),
        name="attend",
    )(work, q, do, total, delta, *parts)


def shards(
    queries,
    key_vector_rows,
    value_vector_rows,
    output_gradient,
    key_lists,
    block_counts,
    span_table,
):
    seq_devices, kv_devices = lax.axis_size("seq"), lax.axis_size("kvh")
    seq_at, kv_at = lax.axis_index("seq"), lax.axis_index("kvh")
    per_kvh = key_vector_rows.shape[0]
    half, middles = seq_devices // 2, seq_devices // 4
    span_rows = kv_devices * per_kvh
    near_groups = [
        [
            (top * half + middle * 2 + core) * kv_devices + head
            for middle in range(middles)
            for head in range(kv_devices)
        ]
        for top in range(2)
        for core in range(2)
    ]

    def swap(x, seq_step, kv_step):
        if seq_step == 0 and kv_step == 0:
            return x
        pairs = [
            (s * kv_devices + h, (s ^ seq_step) * kv_devices + (h ^ kv_step))
            for s in range(seq_devices)
            for h in range(kv_devices)
        ]
        return lax.ppermute(x, ("seq", "kvh"), pairs)

    def exchange_near(x):
        x = x.reshape(middles * kv_devices, per_kvh, 2 * HEAD)
        return lax.all_to_all(x, ("seq", "kvh"), 0, 0, axis_index_groups=near_groups)

    work = resolve(key_lists.T, block_counts, span_table, queries.shape[0] // BLOCK, per_kvh)
    own = jnp.stack(
        [
            jnp.concatenate([x[:, h * HEAD : (h + 1) * HEAD] for x in (key_vector_rows, value_vector_rows)], 1)
            for h in range(kv_devices)
        ]
    )
    far = swap(own, half, 0)
    mine = [lax.dynamic_index_in_dim(own, kv_at ^ j, 0, False) for j in range(kv_devices)]
    near_span = jnp.concatenate([swap(mine[j], 0, j) for j in range(kv_devices)], 0)
    near_part = jnp.concatenate([swap(near_span, 2 * m, 0) for m in range(middles)], 0)
    near_pair = swap(near_part, 1, 0)
    far, work = lax.optimization_barrier((far, work))
    far_part = exchange_near(jnp.broadcast_to(far[None], (middles, *far.shape)))
    far_part = far_part.reshape(near_part.shape)

    common = (per_kvh, work, queries, output_gradient)
    total, delta = near_sums(*common, near_part, near_pair)
    total, far_part = lax.optimization_barrier((total, far_part))
    far_pair = swap(far_part, 1, 0)
    dqt, *partials = attend(*common, total, delta, [near_part, near_pair, far_part, far_pair])

    def chip_rows(kept, received, m):
        rows = slice(m * span_rows, (m + 1) * span_rows)
        return kept[rows].astype(F32) + received[rows].astype(F32)

    def sent_to_middles(kept, received):
        return [swap(chip_rows(kept, received, m).astype(BF16), 2 * m, 0) for m in range(1, middles)]

    def added(kept, received, others):
        return sum([x.astype(F32) for x in others], chip_rows(kept, received, 0))

    def to_owners(span, seq_step):
        pieces = [span[j * per_kvh : (j + 1) * per_kvh] for j in range(kv_devices)]
        return [
            x if seq_step + j == 0 else swap(x.astype(BF16), seq_step, j).astype(F32)
            for j, x in enumerate(pieces)
        ]

    far_received, near_received = swap(partials[3], 1, 0), swap(partials[1], 1, 0)
    far_others = sent_to_middles(partials[2], far_received)
    near_others = sent_to_middles(partials[0], near_received)
    far_span_sums = added(partials[2], far_received, far_others).astype(BF16)
    dqt, far_span_sums = lax.optimization_barrier((dqt, far_span_sums))
    dq = jnp.transpose(dqt.reshape(-1, HEAD, GROUP, BLOCK), (0, 3, 2, 1)) * SCALE
    grad_queries = dq.reshape(queries.shape).astype(BF16)
    far_sums = to_owners(far_span_sums, half)
    near_grads = to_owners(added(partials[0], near_received, near_others), 0)
    sums = jnp.stack([x + y for x, y in zip(near_grads, far_sums)])
    sums = [lax.dynamic_index_in_dim(sums, kv_at ^ h, 0, False) for h in range(kv_devices)]
    key_gradient = jnp.concatenate([x[:, :HEAD] * SCALE for x in sums], 1).astype(BF16)
    value_gradient = jnp.concatenate([x[:, HEAD:] for x in sums], 1).astype(BF16)
    return grad_queries, key_gradient, value_gradient


def solution(mesh):
    placed = (
        P("seq", "kvh"),
        P(("seq", "kvh"), None),
        P(("seq", "kvh"), None),
        P("seq", "kvh"),
        P(),
        P(),
        P(),
    )
    return jax.shard_map(
        shards,
        mesh=mesh,
        in_specs=placed,
        out_specs=(P("seq", "kvh"), P(("seq", "kvh"), None), P(("seq", "kvh"), None)),
        check_vma=False,
    )
```
